32 devices in a mesh: blk: 8 (over y, x, core), row: 4 (over z).
Axes of the slice: x: 2, y: 2, z: 4, core: 2. Of those that a mesh axis runs over, the one named last changes fastest.
Arguments:
- gauss_params: float32 [14, 16384], P(None, ('blk', 'row')), may hold values from -7 to 10, as said below
- tile_ids: int32 [512], P(('blk', 'row')), may hold values from 0 to 511, as said below
- tile_lists: int32 [512, 1024], P(('blk', 'row')), may hold values from -1 to 16383, as said below
Outputs:
- pixel_colors: float32 [512, 3, 256], P(('blk', 'row'))
- transmittance: float32 [512, 256], P(('blk', 'row'))
- significance: float32 [16384], P(('blk', 'row'))
The draws below stay inside these ranges and needn't reach their ends.
Inputs may be any that keep to these rules, and one draw needn't show every extreme that they name: `gauss_params`: rows 0 to 2 are a mean in camera coordinates whose z lies between 2 and 10; rows 3 to 5 are logarithms of scales; rows 6 to 9 a quaternion (w, x, y, z) with w between 0.5 and 1.5 and the others between -1 and 1; row 10 an opacity logit; rows 11 to 13 color coefficients. `tile_ids`: each of the 512 window tiles is held by exactly one slot. `tile_lists`: A list holds distinct Gaussian indices in ascending order of the mean's z, followed by -1 entries. The lists of the 16 slots of one device name at most 200 distinct indices of any one block s * 512 to (s + 1) * 512 - 1, and some device names exactly 200 of some block.
All inputs are finite; a program needn't handle non-finite values.
Results may differ from the reference program's by a relative error of at most 0.0003.
Values sent between devices are 32-bit elements; how exact they have to be, the bound alone decides.
No kernel may reach another device: no remote copies, remote signals or barrier semaphores. Data moves between devices by JAX's collectives and lax.ppermute only.
A program may use at most 128 MiB of HBM per device.

```python
import jax
import jax.numpy as jnp
from jax import lax

TILE_SIDE = 16
SCREEN_W = 3840
SCREEN_H = 2160
WIN_X = 64
TILES_DEV = 16
PER_TILE = 32
RADIUS = 2
LIST = 1024
BLOCK = 256
TILES = 512
WIN_Y = 8
G_DEV = 512
GAUSS = 16384
CAP = 200


FOCAL = 3200.0


def shared_layout(key):
    depth_rank = jax.random.permutation(jax.random.fold_in(key, 11), GAUSS).astype(jnp.int32)
    density = jax.random.randint(jax.random.fold_in(key, 12), (TILES,), PER_TILE // 4, PER_TILE + 1).astype(jnp.int32)
    owners = jax.random.permutation(jax.random.fold_in(key, 13), TILES).astype(jnp.int32)
    labels = jax.random.permutation(jax.random.fold_in(key, 14), GAUSS).astype(jnp.int32)
    return (depth_rank, density, owners, labels)


def draw_tile_ids(key, part):
    depth_rank, density, owners, labels = shared_layout(key)
    return owners


def draw_tile_lists(key, part):
    depth_rank, density, owners, labels = shared_layout(key)
    win_y = TILES // WIN_X
    reach = 2 * RADIUS + 1
    tile_index = jnp.arange(TILES, dtype=jnp.int32)
    offsets = jnp.arange(-RADIUS, RADIUS + 1, dtype=jnp.int32)
    near_col = (tile_index % WIN_X)[:, None, None, None] + offsets[None, :, None, None]
    near_row = (tile_index // WIN_X)[:, None, None, None] + offsets[None, None, :, None]
    level_index = jnp.arange(PER_TILE, dtype=jnp.int32)[None, None, None, :]
    inside = (near_col >= 0) & (near_col < WIN_X) & (near_row >= 0) & (near_row < win_y)
    neighbour = jnp.clip(near_row, 0, win_y - 1) * WIN_X + jnp.clip(near_col, 0, WIN_X - 1)
    is_live = inside & (level_index < density[neighbour])
    gauss_index = level_index * TILES + neighbour
    span = reach * reach * PER_TILE
    gauss_index = jnp.broadcast_to(gauss_index, (TILES, reach, reach, PER_TILE)).reshape(TILES, span)
    is_live = jnp.broadcast_to(is_live, (TILES, reach, reach, PER_TILE)).reshape(TILES, span)
    sort_key = jnp.where(is_live, depth_rank[gauss_index], GAUSS + jnp.arange(span, dtype=jnp.int32)[None, :])
    sort_order = jnp.argsort(sort_key, axis=1)
    picked = jnp.take_along_axis(gauss_index, sort_order, axis=1)
    kept_mask = jnp.take_along_axis(is_live, sort_order, axis=1)
    full_lists = jnp.where(kept_mask, labels[picked], -1)
    full_lists = jnp.pad(full_lists, ((0, 0), (0, LIST - span)), constant_values=-1)
    slot_lists = full_lists[owners].astype(jnp.int32)
    devices = TILES // TILES_DEV
    slot_device = (jnp.arange(TILES, dtype=jnp.int32) // TILES_DEV)[:, None]
    live = slot_lists >= 0
    flat_index = jnp.where(live, slot_device * GAUSS + slot_lists, devices * GAUSS).astype(jnp.int32)
    wanted = jnp.zeros((devices * GAUSS,), jnp.int32).at[flat_index].set(1, mode='drop')
    ranks = jnp.cumsum(wanted.reshape(devices * devices, G_DEV), axis=1).reshape(-1)
    allowed = (wanted > 0) & (ranks <= CAP)
    kept = live & allowed[jnp.clip(flat_index, 0, devices * GAUSS - 1)]
    position = jnp.arange(LIST, dtype=jnp.int32)[None, :]
    order = jnp.argsort(jnp.where(kept, position, LIST + position), axis=1)
    compact = jnp.take_along_axis(jnp.where(kept, slot_lists, -1), order, axis=1)
    return compact.astype(jnp.int32)


def draw_gauss_params(key, part):
    depth_rank, density, owners, labels = shared_layout(key)
    win_y = TILES // WIN_X
    off_x = (SCREEN_W - WIN_X * TILE_SIDE) // 2
    off_y = (SCREEN_H - win_y * TILE_SIDE) // 2
    gauss_index = jnp.arange(GAUSS, dtype=jnp.int32)
    home_tile = gauss_index % TILES
    sub_keys = jax.random.split(jax.random.fold_in(key, 21), 6)
    jitter = jax.random.uniform(sub_keys[0], (3, GAUSS), jnp.float32)
    depth_z = 2.0 + 8.0 * (depth_rank.astype(jnp.float32) + jitter[0]) / GAUSS
    screen_x = off_x + (home_tile % WIN_X).astype(jnp.float32) * TILE_SIDE + TILE_SIDE * (2.0 * jitter[1] - 0.5)
    screen_y = off_y + (home_tile // WIN_X).astype(jnp.float32) * TILE_SIDE + TILE_SIDE * (2.0 * jitter[2] - 0.5)
    mean_x = (screen_x - SCREEN_W / 2) * depth_z / FOCAL
    mean_y = (screen_y - SCREEN_H / 2) * depth_z / FOCAL
    footprint = jnp.exp(jax.random.uniform(sub_keys[1], (3, GAUSS), jnp.float32, jnp.log(2.0), jnp.log(8.0)))
    logit = jax.random.uniform(sub_keys[3], (1, GAUSS), jnp.float32, -3.0, 7.0)
    log_scales = jnp.log(footprint * depth_z[None, :] / FOCAL)
    quat_w = jax.random.uniform(sub_keys[2], (1, GAUSS), jnp.float32, 0.5, 1.5)
    quat_rest = jax.random.uniform(sub_keys[4], (3, GAUSS), jnp.float32, -1.0, 1.0)
    coeffs = jax.random.uniform(sub_keys[5], (3, GAUSS), jnp.float32, -2.5, 2.5)
    means = jnp.stack([mean_x, mean_y, depth_z])
    natural = jnp.concatenate([means, log_scales, quat_w, quat_rest, logit, coeffs], axis=0).astype(jnp.float32)
    return jnp.zeros((14, GAUSS), jnp.float32).at[:, labels].set(natural)


def setup_inputs(seed: int = 0) -> dict:
    keys = jax.random.split(jax.random.key(seed), 4)
    return {
        "gauss_params": draw_gauss_params(jax.random.fold_in(keys[3], 71), 0),
        "tile_ids": draw_tile_ids(jax.random.fold_in(keys[3], 71), 0),
        "tile_lists": draw_tile_lists(jax.random.fold_in(keys[3], 71), 0),
    }


FOCAL = 3200.0
DILATION = 0.3
SH_ZERO = 0.28209479177387814
ALPHA_CAP = 0.99

def project(params):
    mean_x = params[0]
    mean_y = params[1]
    mean_z = params[2]
    scales = jnp.exp(params[3:6])
    quaternion = params[6:10]
    quaternion = quaternion / jnp.sqrt(lax.optimization_barrier(jnp.sum(quaternion * quaternion, axis=0)))
    quat_w = quaternion[0]
    quat_x = quaternion[1]
    quat_y = quaternion[2]
    quat_z = quaternion[3]
    rotation = [[1.0 - 2.0 * (quat_y * quat_y + quat_z * quat_z), 2.0 * (quat_x * quat_y - quat_w * quat_z), 2.0 * (quat_x * quat_z + quat_w * quat_y)], [2.0 * (quat_x * quat_y + quat_w * quat_z), 1.0 - 2.0 * (quat_x * quat_x + quat_z * quat_z), 2.0 * (quat_y * quat_z - quat_w * quat_x)], [2.0 * (quat_x * quat_z - quat_w * quat_y), 2.0 * (quat_y * quat_z + quat_w * quat_x), 1.0 - 2.0 * (quat_x * quat_x + quat_y * quat_y)]]
    inv_z = 1.0 / mean_z
    jac_a = FOCAL * inv_z
    jac_x = -FOCAL * mean_x * inv_z * inv_z
    jac_y = -FOCAL * mean_y * inv_z * inv_z
    first_row = [(jac_a * rotation[0][column_k] + jac_x * rotation[2][column_k]) * scales[column_k] for column_k in range(3)]
    second_row = [(jac_a * rotation[1][column_k] + jac_y * rotation[2][column_k]) * scales[column_k] for column_k in range(3)]
    cov_a = first_row[0] * first_row[0] + first_row[1] * first_row[1] + first_row[2] * first_row[2] + DILATION
    cov_b = first_row[0] * second_row[0] + first_row[1] * second_row[1] + first_row[2] * second_row[2]
    cov_c = second_row[0] * second_row[0] + second_row[1] * second_row[1] + second_row[2] * second_row[2] + DILATION
    determinant = cov_a * cov_c - cov_b * cov_b
    center_u = FOCAL * mean_x * inv_z + SCREEN_W / 2
    center_v = FOCAL * mean_y * inv_z + SCREEN_H / 2
    opacity = jax.nn.sigmoid(params[10])
    radiance = jnp.maximum(SH_ZERO * params[11:14] + 0.5, 0.0)
    shape_rows = jnp.stack([center_u, center_v, cov_c / determinant, -cov_b / determinant, cov_a / determinant, opacity])
    return jnp.concatenate([shape_rows, radiance], axis=0)

def pixel_grid(tile_ids, off_x, off_y):
    column = (tile_ids % WIN_X).astype(jnp.float32)
    tile_row = (tile_ids // WIN_X).astype(jnp.float32)
    within = jnp.arange(TILE_SIDE * TILE_SIDE, dtype=jnp.int32)
    inner_x = (within % TILE_SIDE).astype(jnp.float32)
    inner_y = (within // TILE_SIDE).astype(jnp.float32)
    pixel_x = off_x + column[:, None] * TILE_SIDE + inner_x[None, :] + 0.5
    pixel_y = off_y + tile_row[:, None] * TILE_SIDE + inner_y[None, :] + 0.5
    return (pixel_x, pixel_y)

def blend_block(carry_state, block_rec, pixel_x, pixel_y):
    transmit, radiance = carry_state
    delta_x = pixel_x[:, :, None] - block_rec[0][:, None, :]
    delta_y = pixel_y[:, :, None] - block_rec[1][:, None, :]
    exponent = -0.5 * (block_rec[2][:, None, :] * delta_x * delta_x + block_rec[4][:, None, :] * delta_y * delta_y) - block_rec[3][:, None, :] * delta_x * delta_y
    alphas = jnp.minimum(ALPHA_CAP, block_rec[5][:, None, :] * jnp.exp(exponent))
    log_keep = jnp.log1p(-alphas)
    before = jnp.cumsum(log_keep, axis=2) - log_keep
    weight = transmit[:, :, None] * jnp.exp(before) * alphas
    radiance = radiance + jnp.einsum('npg,cng->ncp', weight, block_rec[6:9], precision=lax.Precision.HIGHEST)
    transmit = transmit * jnp.exp(lax.optimization_barrier(jnp.sum(log_keep, axis=2)))
    return ((transmit, radiance), lax.optimization_barrier(jnp.sum(weight, axis=1)) / weight.shape[1])

def render_group(operands):
    tables, pixel_x, pixel_y = operands
    count_here = tables.shape[1]
    pixels = pixel_x.shape[1]
    carry_state = (jnp.ones((count_here, pixels), jnp.float32), jnp.zeros((count_here, 3, pixels), jnp.float32))
    block_sums = []
    for block_index in range(tables.shape[2] // BLOCK):
        block_rec = tables[:, :, block_index * BLOCK:(block_index + 1) * BLOCK]
        carry_state, block_sum = blend_block(carry_state, block_rec, pixel_x, pixel_y)
        block_sums.append(block_sum)
    return (carry_state[1], carry_state[0], jnp.concatenate(block_sums, axis=1))

def render(entry_table, tile_ids, off_x, off_y):
    pixel_x, pixel_y = pixel_grid(tile_ids, off_x, off_y)
    tile_count = entry_table.shape[1]
    list_len = entry_table.shape[2]
    grouping = 4
    groups = tile_count // grouping
    grouped = entry_table.reshape(9, groups, grouping, list_len).transpose(1, 0, 2, 3)
    shaped_x = pixel_x.reshape(groups, grouping, -1)
    shaped_y = pixel_y.reshape(groups, grouping, -1)
    radiance, transmit, weight_sums = lax.map(render_group, (grouped, shaped_x, shaped_y))
    return (radiance.reshape(tile_count, 3, -1), transmit.reshape(tile_count, -1), weight_sums.reshape(tile_count, list_len))

def reference(gauss_params, tile_ids, tile_lists):
    records = project(gauss_params)
    is_live = tile_lists >= 0
    safe_ids = jnp.where(is_live, tile_lists, 0)
    entry_table = jnp.where(is_live[None], records[:, safe_ids], 0.0)
    off_x = (SCREEN_W - WIN_X * TILE_SIDE) // 2
    off_y = (SCREEN_H - WIN_Y * TILE_SIDE) // 2
    pixel_colors, transmittance, weight_sums = render(entry_table, tile_ids, off_x, off_y)
    seg_ids = jnp.where(is_live, tile_lists, GAUSS).reshape(-1)
    significance = jax.ops.segment_sum(weight_sums.reshape(-1), seg_ids, num_segments=GAUSS + 1)[:GAUSS]
    return (pixel_colors, transmittance, significance)
```

```python
import functools

import jax
import jax.numpy as jnp
from jax import lax
from jax.experimental import pallas as pl
from jax.experimental.pallas import tpu as pltpu
from jax.sharding import PartitionSpec as P

TILE_SIDE = 16
SCREEN_W = 3840
SCREEN_H = 2160
WIN_X = 64
PIXELS = TILE_SIDE * TILE_SIDE
CHUNK = 256
FIELDS = 9
REC_ROWS = 40
PIECES = (3, 3, 2, 2, 2, 2, 2, 2, 2)
PIECE_AT = tuple(sum(PIECES[:f]) for f in range(FIELDS + 1))

FOCAL = 3200.0
DILATION = 0.3
SH_ZERO = 0.28209479177387814
ALPHA_CAP = 0.99
LOG2E = 1.4426950408889634
DARK = -200.0


def project_kernel(params_ref, lists_ref, rec_ref, count_ref):
    def row(index):
        return params_ref[index : index + 1, :]

    mean_x, mean_y, mean_z = row(0), row(1), row(2)
    scales = [jnp.exp(row(3 + k)) for k in range(3)]
    quat = [row(6 + k) for k in range(4)]
    norm = jnp.sqrt(quat[0] * quat[0] + quat[1] * quat[1] + quat[2] * quat[2] + quat[3] * quat[3])
    qw, qx, qy, qz = [q / norm for q in quat]
    rotation = [
        [1.0 - 2.0 * (qy * qy + qz * qz), 2.0 * (qx * qy - qw * qz), 2.0 * (qx * qz + qw * qy)],
        [2.0 * (qx * qy + qw * qz), 1.0 - 2.0 * (qx * qx + qz * qz), 2.0 * (qy * qz - qw * qx)],
        [2.0 * (qx * qz - qw * qy), 2.0 * (qy * qz + qw * qx), 1.0 - 2.0 * (qx * qx + qy * qy)],
    ]
    inv_z = 1.0 / mean_z
    jac_a = FOCAL * inv_z
    jac_x = -FOCAL * mean_x * inv_z * inv_z
    jac_y = -FOCAL * mean_y * inv_z * inv_z
    first = [(jac_a * rotation[0][k] + jac_x * rotation[2][k]) * scales[k] for k in range(3)]
    second = [(jac_a * rotation[1][k] + jac_y * rotation[2][k]) * scales[k] for k in range(3)]
    cov_a = first[0] * first[0] + first[1] * first[1] + first[2] * first[2] + DILATION
    cov_b = first[0] * second[0] + first[1] * second[1] + first[2] * second[2]
    cov_c = second[0] * second[0] + second[1] * second[1] + second[2] * second[2] + DILATION
    determinant = cov_a * cov_c - cov_b * cov_b
    logit = row(10)
    log_opacity = -LOG2E * (jnp.maximum(-logit, 0.0) + jnp.log1p(jnp.exp(-jnp.abs(logit))))
    fields = [
        FOCAL * mean_x * inv_z + SCREEN_W / 2,
        FOCAL * mean_y * inv_z + SCREEN_H / 2,
        (-0.5 * LOG2E) * (cov_c / determinant),
        LOG2E * (cov_b / determinant),
        (-0.5 * LOG2E) * (cov_a / determinant),
        jnp.maximum(log_opacity, DARK),
    ] + [jnp.maximum(SH_ZERO * row(11 + k) + 0.5, 0.0) for k in range(3)]
    rec_ref[...] = jnp.zeros_like(rec_ref)
    for f, value in enumerate(fields):
        for q in range(4):
            rec_ref[4 * f + q : 4 * f + q + 1, :] = value[:, 128 * q : 128 * (q + 1)]
    live = (lists_ref[...] >= 0).astype(jnp.int32)
    count_ref[...] = jnp.broadcast_to(jnp.sum(live, axis=1, keepdims=True), count_ref.shape)


def pieces_of(value, count):
    found = []
    for _ in range(count):
        piece = value.astype(jnp.bfloat16)
        found.append(piece)
        value = value - piece.astype(jnp.float32)
    return found


def render_kernel(
    pair_bit, off_x, off_y, tids_ref, count_ref, mine_ref, other_ref, lists_ref,
    color_ref, trans_ref, sig_ref,
    table_ref, feat_ref, exp0_ref, exp1_ref, w0_ref, w1_ref, rgb_ref, acc_ref, through_ref,
):
    f32, bf16 = jnp.float32, jnp.bfloat16
    tiles = lists_ref.shape[0]
    half = mine_ref.shape[0] // REC_ROWS
    devices = 2 * half
    groups = tiles // 8
    me = lax.axis_index(("blk", "row"))
    my_bit = jnp.bitwise_and(jnp.right_shift(me, pair_bit), 1)

    for f in range(FIELDS):
        for q in range(4):
            for part, ref in enumerate((mine_ref, other_ref)):
                rows = ref[pl.ds(4 * f + q, half, stride=REC_ROWS), :]
                for p, piece in enumerate(pieces_of(rows, PIECES[f])):
                    at = (PIECE_AT[f] + p) * 2 * devices + (q // 2) * devices + part * half
                    table_ref[pl.ds(at, half), pl.ds(128 * (q % 2), 128)] = piece

    pixel = lax.broadcasted_iota(jnp.int32, (8, PIXELS), 1)
    which = lax.broadcasted_iota(jnp.int32, (8, PIXELS), 0)
    px = jnp.bitwise_and(pixel, TILE_SIDE - 1).astype(f32) - 7.5
    py = jnp.right_shift(pixel, 4).astype(f32) - 7.5
    feats = jnp.zeros((8, PIXELS), f32)
    for j, value in enumerate((px * px, px * py, py * py, px, py, jnp.ones_like(px))):
        feats = jnp.where(which == j, value, feats)
    feat_ref[...] = jnp.concatenate([feats, feats, feats, jnp.zeros_like(feats)], axis=0).astype(bf16)

    through_ref[...] = jnp.ones_like(through_ref)
    acc_ref[...] = jnp.zeros_like(acc_ref)
    sig_ref[...] = jnp.zeros_like(sig_ref)
    most = count_ref[0, 0]
    for t in range(1, tiles):
        most = jnp.maximum(most, count_ref[t, 0])

    def ids_of(t, c):
        return lists_ref[pl.ds(t, 1), pl.ds(pl.multiple_of(c * CHUNK, CHUNK), CHUNK)]

    def prepare(t, c):
        ids = ids_of(t, c)
        lane = jnp.bitwise_and(ids, 255)
        owner = jnp.right_shift(ids, 9)
        low = jnp.bitwise_and(owner, (1 << pair_bit) - 1)
        rank = jnp.left_shift(jnp.right_shift(owner, pair_bit + 1), pair_bit) + low
        part = jnp.bitwise_xor(jnp.bitwise_and(jnp.right_shift(owner, pair_bit), 1), my_bit)
        place = jnp.bitwise_and(jnp.right_shift(ids, 8), 1) * devices + part * half + rank
        place = jnp.where(ids >= 0, place, -1)
        onehot = (lax.broadcasted_iota(jnp.int32, (256, CHUNK), 0) == lane).astype(f32).astype(bf16)
        chosen = lax.broadcasted_iota(jnp.int32, (2 * devices, CHUNK), 0) == place

        def fetch(f):
            total = None
            for p in range(PIECE_AT[f], PIECE_AT[f + 1]):
                part = jnp.dot(
                    table_ref[p * 2 * devices : (p + 1) * 2 * devices, :], onehot, preferred_element_type=f32
                )
                total = part if total is None else total + part
            return jnp.sum(jnp.where(chosen, total, 0.0), axis=0, keepdims=True)

        u, v, ca, cb, cc, log_op, red, green, blue = [fetch(f) for f in range(FIELDS)]
        tid = tids_ref[t]
        center_x = (off_x + TILE_SIDE // 2 + TILE_SIDE * jnp.bitwise_and(tid, WIN_X - 1)).astype(f32)
        center_y = (off_y + TILE_SIDE // 2 + TILE_SIDE * jnp.right_shift(tid, 6)).astype(f32)
        du = u - center_x
        dv = v - center_y
        log_op = jnp.where(ids >= 0, log_op, DARK)
        terms = (
            ca,
            cb,
            cc,
            -2.0 * ca * du - cb * dv,
            -2.0 * cc * dv - cb * du,
            ca * du * du + cc * dv * dv + cb * du * dv + log_op,
        )
        row8 = lax.broadcasted_iota(jnp.int32, (8, CHUNK), 0)
        coef = jnp.zeros((8, CHUNK), f32)
        for j, value in enumerate(terms):
            coef = jnp.where(row8 == j, value, coef)
        p0, p1, p2 = [p.astype(f32) for p in pieces_of(coef, 3)]
        coefs = jnp.concatenate([p0, p1, p2, jnp.zeros_like(p0)], axis=0).astype(bf16)
        exponent = lax.dot_general(
            coefs, feat_ref[...], (((0,), (0,)), ((), ())), preferred_element_type=f32
        )
        at = pl.ds(pl.multiple_of(t * CHUNK, CHUNK), CHUNK)
        exp0_ref[at, :] = exponent[:, :128]
        exp1_ref[at, :] = exponent[:, 128:]
        rgb = jnp.zeros((8, CHUNK), f32)
        for j, value in enumerate((red, green, blue)):
            rgb = jnp.where(row8 == j, value, rgb)
        c0, c1 = pieces_of(rgb, 2)
        rgb_ref[pl.ds(pl.multiple_of(t * 16, 16), 16), :] = jnp.concatenate(
            [c0.astype(f32), c1.astype(f32)], axis=0
        ).astype(bf16)

    def blend(step, through):
        for j in range(8):
            k = step * 8 + j
            after = []
            for g in range(groups):
                for h, (e_ref, w_ref) in enumerate(((exp0_ref, w0_ref), (exp1_ref, w1_ref))):
                    at = pl.ds(g * 8 * CHUNK + k, 8, stride=CHUNK)
                    alpha = jnp.minimum(jnp.exp2(e_ref[at, :]), ALPHA_CAP)
                    before = through[2 * g + h]
                    w_ref[at, :] = before * alpha
                    after.append(before * (1.0 - alpha))
            through = tuple(after)
        return through

    def collect(t, c):
        ids = ids_of(t, c)
        at = pl.ds(pl.multiple_of(t * CHUNK, CHUNK), CHUNK)
        weight = jnp.concatenate([w0_ref[at, :], w1_ref[at, :]], axis=1)
        w_hi, w_lo = pieces_of(weight, 2)
        at16 = pl.ds(pl.multiple_of(t * 16, 16), 16)
        rgb = rgb_ref[at16, :]
        acc_ref[at16, :] += jnp.dot(rgb, w_hi, preferred_element_type=f32) + jnp.dot(
            rgb, w_lo, preferred_element_type=f32
        )
        ones = jnp.ones((16, PIXELS), bf16)
        nt = (((1,), (1,)), ((), ()))
        sums = lax.dot_general(ones, w_hi, nt, preferred_element_type=f32) + lax.dot_general(
            ones, w_lo, nt, preferred_element_type=f32
        )
        s0, s1 = pieces_of(sums[0:1, :], 2)
        rows = sig_ref.shape[0]
        hit = lax.broadcasted_iota(jnp.int32, (rows, CHUNK), 0) == jnp.right_shift(ids, 7)
        lanes = (
            lax.broadcasted_iota(jnp.int32, (128, CHUNK), 0) == jnp.bitwise_and(ids, 127)
        ).astype(f32).astype(bf16)
        left = jnp.concatenate(
            [jnp.where(hit, s.astype(f32), 0.0).astype(bf16) for s in (s0, s1)], axis=0
        )
        both = lax.dot_general(left, lanes, nt, preferred_element_type=f32)
        sig_ref[...] += both[:rows] + both[rows:]

    def chunk_body(c, carry):
        def prep_body(t, _):
            active = count_ref[t, 0] > c * CHUNK

            @pl.when(active)
            def _():
                prepare(t, c)

            @pl.when(jnp.logical_not(active))
            def _():
                at = pl.ds(pl.multiple_of(t * CHUNK, CHUNK), CHUNK)
                exp0_ref[at, :] = jnp.full((CHUNK, 128), DARK, f32)
                exp1_ref[at, :] = jnp.full((CHUNK, 128), DARK, f32)

            return 0

        lax.fori_loop(0, tiles, prep_body, 0)
        through = tuple(through_ref[8 * i : 8 * i + 8, :] for i in range(2 * groups))
        through = lax.fori_loop(0, CHUNK // 8, blend, through)
        for i in range(2 * groups):
            through_ref[8 * i : 8 * i + 8, :] = through[i]

        def collect_body(t, _):
            @pl.when(count_ref[t, 0] > c * CHUNK)
            def _():
                collect(t, c)

            return 0

        lax.fori_loop(0, tiles, collect_body, 0)
        return carry

    lax.fori_loop(0, (most + CHUNK - 1) // CHUNK, chunk_body, 0)

    for t in range(tiles):
        color_ref[t] = acc_ref[16 * t : 16 * t + 3, :] + acc_ref[16 * t + 8 : 16 * t + 11, :]
    for g in range(groups):
        for h in range(2):
            i = 2 * g + h
            trans_ref[8 * g : 8 * g + 8, 128 * h : 128 * (h + 1)] = through_ref[8 * i : 8 * i + 8, :]
    sig_ref[...] = sig_ref[...] * (1.0 / PIXELS)


def local(pair_bit, gauss_params, tile_ids, tile_lists):
    axes = ("blk", "row")
    devices = lax.axis_size(axes)
    tiles_here, list_len = tile_lists.shape
    half = devices // 2
    records, counts = pl.pallas_call(
        project_kernel,
        out_shape=(
            jax.ShapeDtypeStruct((REC_ROWS, 128), jnp.float32),
            jax.ShapeDtypeStruct((tiles_here, 128), jnp.int32),
        ),
    )(gauss_params, tile_lists)
    bit = 1 << pair_bit
    members = [[d for d in range(devices) if (d & bit) == part * bit] for part in range(2)]
    mine = lax.all_to_all(
        jnp.broadcast_to(records[None], (half, REC_ROWS, 128)), axes, 0, 0, axis_index_groups=members
    ).reshape(half * REC_ROWS, 128)
    other = lax.ppermute(mine, axes, [(d, d ^ bit) for d in range(devices)])

    tiles_total = tiles_here * devices
    win_y = tiles_total // WIN_X
    off_x = (SCREEN_W - WIN_X * TILE_SIDE) // 2
    off_y = (SCREEN_H - win_y * TILE_SIDE) // 2
    sig_rows = devices * gauss_params.shape[1] // 128
    vmem = pl.BlockSpec(memory_space=pltpu.VMEM)
    smem = pl.BlockSpec(memory_space=pltpu.SMEM)
    pixel_colors, transmittance, partial_sig = pl.pallas_call(
        functools.partial(render_kernel, pair_bit, off_x, off_y),
        out_shape=(
            jax.ShapeDtypeStruct((tiles_here, 3, PIXELS), jnp.float32),
            jax.ShapeDtypeStruct((tiles_here, PIXELS), jnp.float32),
            jax.ShapeDtypeStruct((sig_rows, 128), jnp.float32),
        ),
        in_specs=[smem, smem, vmem, vmem, vmem],
        out_specs=(vmem, vmem, vmem),
        scratch_shapes=[
            pltpu.VMEM((PIECE_AT[-1] * 2 * devices, 256), jnp.bfloat16),
            pltpu.VMEM((32, PIXELS), jnp.bfloat16),
            pltpu.VMEM((tiles_here * CHUNK, 128), jnp.float32),
            pltpu.VMEM((tiles_here * CHUNK, 128), jnp.float32),
            pltpu.VMEM((tiles_here * CHUNK, 128), jnp.float32),
            pltpu.VMEM((tiles_here * CHUNK, 128), jnp.float32),
            pltpu.VMEM((tiles_here * 16, CHUNK), jnp.bfloat16),
            pltpu.VMEM((tiles_here * 16, PIXELS), jnp.float32),
            pltpu.VMEM((tiles_here * 2, 128), jnp.float32),
        ],
        compiler_params=pltpu.CompilerParams(vmem_limit_bytes=48 * 2**20),
    )(tile_ids, counts, mine, other, tile_lists)
    swapped = lax.all_to_all(partial_sig.reshape(devices, -1, 128), axes, 0, 0)
    significance = jnp.sum(swapped, axis=0).reshape(-1)
    return (pixel_colors, transmittance, significance)


def pair_bit_of(mesh):
    flat = list(mesh.devices.flat)
    bit = 0
    while (2 << bit) <= len(flat):
        if getattr(flat[0], "coords", 0) == getattr(flat[1 << bit], "coords", 1):
            return bit
        bit += 1
    return 0


def solution(mesh):
    return jax.shard_map(
        functools.partial(local, pair_bit_of(mesh)),
        mesh=mesh,
        in_specs=(P(None, ("blk", "row")), P(("blk", "row")), P(("blk", "row"), None)),
        out_specs=(P(("blk", "row"), None, None), P(("blk", "row"), None), P(("blk", "row"))),
        check_vma=False,
    )
```

```python
import functools

import jax
import jax.numpy as jnp
from jax import lax
from jax.experimental import pallas as pl
from jax.experimental.pallas import tpu as pltpu
from jax.sharding import PartitionSpec as P

TILE_SIDE = 16
SCREEN_W = 3840
SCREEN_H = 2160
WIN_X = 64
PIXELS = TILE_SIDE * TILE_SIDE
CHUNK = 256
STRIDE = CHUNK + 8
UNROLL = 8
FIELDS = 9
REC_ROWS = 40
PIECES = (3, 3, 2, 2, 2, 2, 2, 2, 2)
PIECE_AT = tuple(sum(PIECES[:f]) for f in range(FIELDS + 1))

FOCAL = 3200.0
DILATION = 0.3
SH_ZERO = 0.28209479177387814
ALPHA_CAP = 0.99
LOG2E = 1.4426950408889634
DARK = -200.0


def project_kernel(params_ref, lists_ref, rec_ref, count_ref):
    def row(index):
        return params_ref[index : index + 1, :]

    mean_x, mean_y, mean_z = row(0), row(1), row(2)
    scales = [jnp.exp(row(3 + k)) for k in range(3)]
    quat = [row(6 + k) for k in range(4)]
    norm = jnp.sqrt(quat[0] * quat[0] + quat[1] * quat[1] + quat[2] * quat[2] + quat[3] * quat[3])
    qw, qx, qy, qz = [q / norm for q in quat]
    rotation = [
        [1.0 - 2.0 * (qy * qy + qz * qz), 2.0 * (qx * qy - qw * qz), 2.0 * (qx * qz + qw * qy)],
        [2.0 * (qx * qy + qw * qz), 1.0 - 2.0 * (qx * qx + qz * qz), 2.0 * (qy * qz - qw * qx)],
        [2.0 * (qx * qz - qw * qy), 2.0 * (qy * qz + qw * qx), 1.0 - 2.0 * (qx * qx + qy * qy)],
    ]
    inv_z = 1.0 / mean_z
    jac_a = FOCAL * inv_z
    jac_x = -FOCAL * mean_x * inv_z * inv_z
    jac_y = -FOCAL * mean_y * inv_z * inv_z
    first = [(jac_a * rotation[0][k] + jac_x * rotation[2][k]) * scales[k] for k in range(3)]
    second = [(jac_a * rotation[1][k] + jac_y * rotation[2][k]) * scales[k] for k in range(3)]
    cov_a = first[0] * first[0] + first[1] * first[1] + first[2] * first[2] + DILATION
    cov_b = first[0] * second[0] + first[1] * second[1] + first[2] * second[2]
    cov_c = second[0] * second[0] + second[1] * second[1] + second[2] * second[2] + DILATION
    determinant = cov_a * cov_c - cov_b * cov_b
    logit = row(10)
    log_opacity = -LOG2E * (jnp.maximum(-logit, 0.0) + jnp.log1p(jnp.exp(-jnp.abs(logit))))
    fields = [
        FOCAL * mean_x * inv_z + SCREEN_W / 2,
        FOCAL * mean_y * inv_z + SCREEN_H / 2,
        (-0.5 * LOG2E) * (cov_c / determinant),
        LOG2E * (cov_b / determinant),
        (-0.5 * LOG2E) * (cov_a / determinant),
        jnp.maximum(log_opacity, DARK),
    ] + [jnp.maximum(SH_ZERO * row(11 + k) + 0.5, 0.0) for k in range(3)]
    rec_ref[...] = jnp.zeros_like(rec_ref)
    for f, value in enumerate(fields):
        for q in range(4):
            rec_ref[4 * f + q : 4 * f + q + 1, :] = value[:, 128 * q : 128 * (q + 1)]
    live = (lists_ref[...] >= 0).astype(jnp.int32)
    count_ref[...] = jnp.broadcast_to(jnp.sum(live, axis=1, keepdims=True), count_ref.shape)


def pieces_of(value, count):
    found = []
    for _ in range(count):
        piece = value.astype(jnp.bfloat16)
        found.append(piece)
        value = value - piece.astype(jnp.float32)
    return found


def render_kernel(
    pair_bit, off_x, off_y, tids_ref, count_ref, mine_ref, other_ref, lists_ref,
    color_ref, trans_ref, sig_ref,
    table_ref, feat_ref, exp0_ref, exp1_ref, w0_ref, w1_ref, rgb_ref, acc_ref, through_ref,
    ids_ref, coef_ref, slot_ref,
):
    f32, bf16 = jnp.float32, jnp.bfloat16
    tiles = lists_ref.shape[0]
    half = mine_ref.shape[0] // REC_ROWS
    devices = 2 * half
    groups = tiles // 8
    me = lax.axis_index(("blk", "row"))
    my_bit = jnp.bitwise_and(jnp.right_shift(me, pair_bit), 1)

    for f in range(FIELDS):
        for q in range(4):
            for part, ref in enumerate((mine_ref, other_ref)):
                rows = ref[pl.ds(4 * f + q, half, stride=REC_ROWS), :]
                for p, piece in enumerate(pieces_of(rows, PIECES[f])):
                    at = (PIECE_AT[f] + p) * 2 * devices + (q // 2) * devices + part * half
                    table_ref[pl.ds(at, half), pl.ds(128 * (q % 2), 128)] = piece

    pixel = lax.broadcasted_iota(jnp.int32, (8, PIXELS), 1)
    which = lax.broadcasted_iota(jnp.int32, (8, PIXELS), 0)
    px = jnp.bitwise_and(pixel, TILE_SIDE - 1).astype(f32) - 7.5
    py = jnp.right_shift(pixel, 4).astype(f32) - 7.5
    feats = jnp.zeros((8, PIXELS), f32)
    for j, value in enumerate((px * px, px * py, py * py, px, py, jnp.ones_like(px))):
        feats = jnp.where(which == j, value, feats)
    feat_ref[...] = jnp.concatenate([feats, feats, feats, jnp.zeros_like(feats)], axis=0).astype(bf16)

    through_ref[...] = jnp.ones_like(through_ref)
    acc_ref[...] = jnp.zeros_like(acc_ref)
    sig_ref[...] = jnp.zeros_like(sig_ref)
    most = count_ref[0, 0]
    for t in range(1, tiles):
        most = jnp.maximum(most, count_ref[t, 0])

    def ids_of(t, c):
        return ids_ref[pl.ds(t, 1), pl.ds(pl.multiple_of(c * CHUNK, CHUNK), CHUNK)]

    def slot(t):
        return pl.ds(pl.multiple_of(t * STRIDE, 8), CHUNK)

    def one_hot(rows, index):
        iota = lax.broadcasted_iota(jnp.int32, (rows, index.shape[1]), 0)
        return (iota == index).astype(f32).astype(bf16)

    def prepare(t, c):
        ids = ids_of(t, c)
        owner = jnp.right_shift(ids, 9)
        low = jnp.bitwise_and(owner, (1 << pair_bit) - 1)
        rank = jnp.left_shift(jnp.right_shift(owner, pair_bit + 1), pair_bit) + low
        part = jnp.bitwise_xor(jnp.bitwise_and(jnp.right_shift(owner, pair_bit), 1), my_bit)
        place = jnp.bitwise_and(jnp.right_shift(ids, 8), 1) * devices + part * half + rank
        place = jnp.where(ids >= 0, place, -1)
        chosen = lax.broadcasted_iota(jnp.int32, (2 * devices, CHUNK), 0) == place
        looked = jnp.dot(table_ref[...], one_hot(256, jnp.bitwise_and(ids, 255)), preferred_element_type=f32)

        def fetch(f):
            total = None
            for p in range(PIECE_AT[f], PIECE_AT[f + 1]):
                piece = looked[p * 2 * devices : (p + 1) * 2 * devices]
                total = piece if total is None else total + piece
            return jnp.sum(jnp.where(chosen, total, 0.0), axis=0, keepdims=True)

        u, v, ca, cb, cc, log_op, red, green, blue = [fetch(f) for f in range(FIELDS)]
        tid = tids_ref[jnp.minimum(t, tiles - 1)]
        center_x = (off_x + TILE_SIDE // 2 + TILE_SIDE * jnp.bitwise_and(tid, WIN_X - 1)).astype(f32)
        center_y = (off_y + TILE_SIDE // 2 + TILE_SIDE * jnp.right_shift(tid, 6)).astype(f32)
        du = u - center_x
        dv = v - center_y
        log_op = jnp.where(ids >= 0, log_op, DARK)
        terms = (
            ca,
            cb,
            cc,
            -2.0 * ca * du - cb * dv,
            -2.0 * cc * dv - cb * du,
            ca * du * du + cc * dv * dv + cb * du * dv + log_op,
        )
        row8 = lax.broadcasted_iota(jnp.int32, (8, CHUNK), 0)
        coef = jnp.zeros((8, CHUNK), f32)
        for j, value in enumerate(terms):
            coef = jnp.where(row8 == j, value, coef)
        p0, p1, p2 = [p.astype(f32) for p in pieces_of(coef, 3)]
        coef_ref[pl.ds(pl.multiple_of(t * 32, 32), 32), :] = jnp.concatenate(
            [p0, p1, p2, jnp.zeros_like(p0)], axis=0
        ).astype(bf16)
        rgb = jnp.zeros((8, CHUNK), f32)
        for j, value in enumerate((red, green, blue)):
            rgb = jnp.where(row8 == j, value, rgb)
        c0, c1 = pieces_of(rgb, 2)
        rgb_ref[pl.ds(pl.multiple_of(t * 16, 16), 16), :] = jnp.concatenate(
            [c0.astype(f32), c1.astype(f32)], axis=0
        ).astype(bf16)

    def exponents(t):
        exponent = lax.dot_general(
            coef_ref[pl.ds(pl.multiple_of(t * 32, 32), 32), :], feat_ref[...],
            (((0,), (0,)), ((), ())), preferred_element_type=f32,
        )
        exp0_ref[slot(t), :] = exponent[:, :128]
        exp1_ref[slot(t), :] = exponent[:, 128:]

    def blend(step, through):
        for j in range(8):
            k = step * 8 + j
            after = []
            for g in range(groups):
                for h, (e_ref, w_ref) in enumerate(((exp0_ref, w0_ref), (exp1_ref, w1_ref))):
                    at = pl.ds(g * 8 * STRIDE + k, 8, stride=STRIDE)
                    alpha = jnp.minimum(jnp.exp2(e_ref[at, :]), ALPHA_CAP)
                    before = through[2 * g + h]
                    w_ref[at, :] = before * alpha
                    after.append(before * (1.0 - alpha))
            through = tuple(after)
        return through

    def collect(slots, c):
        left, right = [], []
        for t in slots:
            ids = ids_of(t, c)
            w0, w1 = w0_ref[slot(t), :], w1_ref[slot(t), :]
            high, low = pieces_of(jnp.concatenate([w0, w1], axis=1), 2)
            at16 = pl.ds(pl.multiple_of(t * 16, 16), 16)
            rgb = rgb_ref[at16, :]
            acc_ref[at16, :] += jnp.dot(rgb, high, preferred_element_type=f32) + jnp.dot(
                rgb, low, preferred_element_type=f32
            )
            sums = jnp.sum(w0 + w1, axis=1, keepdims=True)
            inner = jnp.bitwise_and(ids, 127)
            columns = jnp.concatenate(
                [
                    jnp.broadcast_to(inner[:, 128 * i : 128 * (i + 1)], (128, 128)).T
                    for i in range(CHUNK // 128)
                ],
                axis=0,
            )
            spread = jnp.where(lax.broadcasted_iota(jnp.int32, (CHUNK, 128), 1) == columns, sums, 0.0)
            right.append(jnp.concatenate(pieces_of(spread, 2), axis=1))
            left.append(one_hot(sig_ref.shape[0], jnp.right_shift(ids, 7)))
        both = jnp.dot(
            jnp.concatenate(left, axis=1), jnp.concatenate(right, axis=0), preferred_element_type=f32
        )
        sig_ref[...] += both[:, :128] + both[:, 128:]

    def chunk_body(c, carry):
        found = jnp.int32(0)
        for t in range(tiles):
            slot_ref[found] = t
            found += (count_ref[t, 0] > c * CHUNK).astype(jnp.int32)
        for i in range(UNROLL):
            slot_ref[found + i] = tiles
        rounds = (found + UNROLL - 1) // UNROLL

        def prep_body(i, _):
            for j in range(UNROLL):
                prepare(slot_ref[i * UNROLL + j], c)
            return 0

        def exponent_body(i, _):
            for j in range(UNROLL):
                exponents(slot_ref[i * UNROLL + j])
            return 0

        def dark_body(t, _):
            @pl.when(count_ref[t, 0] <= c * CHUNK)
            def _():
                exp0_ref[slot(t), :] = jnp.full((CHUNK, 128), DARK, f32)
                exp1_ref[slot(t), :] = jnp.full((CHUNK, 128), DARK, f32)

            return 0

        lax.fori_loop(0, tiles, dark_body, 0)
        lax.fori_loop(0, rounds, prep_body, 0)
        lax.fori_loop(0, rounds, exponent_body, 0)
        through = tuple(through_ref[8 * i : 8 * i + 8, :] for i in range(2 * groups))
        through = lax.fori_loop(0, CHUNK // 8, blend, through)
        for i in range(2 * groups):
            through_ref[8 * i : 8 * i + 8, :] = through[i]

        def collect_body(i, _):
            collect([slot_ref[i * UNROLL + j] for j in range(UNROLL)], c)
            return 0

        lax.fori_loop(0, rounds, collect_body, 0)
        return carry

    ids_ref[pl.ds(0, tiles), :] = lists_ref[...]
    ids_ref[pl.ds(tiles, 8), :] = jnp.full((8, lists_ref.shape[1]), -1, jnp.int32)
    w0_ref[slot(tiles), :] = jnp.zeros((CHUNK, 128), f32)
    w1_ref[slot(tiles), :] = jnp.zeros((CHUNK, 128), f32)
    lax.fori_loop(0, (most + CHUNK - 1) // CHUNK, chunk_body, 0)

    for t in range(tiles):
        color_ref[t] = acc_ref[16 * t : 16 * t + 3, :] + acc_ref[16 * t + 8 : 16 * t + 11, :]
    for g in range(groups):
        for h in range(2):
            i = 2 * g + h
            trans_ref[8 * g : 8 * g + 8, 128 * h : 128 * (h + 1)] = through_ref[8 * i : 8 * i + 8, :]
    sig_ref[...] = sig_ref[...] * (1.0 / PIXELS)


def local(pair_bit, gauss_params, tile_ids, tile_lists):
    axes = ("blk", "row")
    devices = lax.axis_size(axes)
    tiles_here, list_len = tile_lists.shape
    half = devices // 2
    records, counts = pl.pallas_call(
        project_kernel,
        out_shape=(
            jax.ShapeDtypeStruct((REC_ROWS, 128), jnp.float32),
            jax.ShapeDtypeStruct((tiles_here, 128), jnp.int32),
        ),
    )(gauss_params, tile_lists)
    bit = 1 << pair_bit
    members = [[d for d in range(devices) if (d & bit) == part * bit] for part in range(2)]
    mine = lax.all_to_all(
        jnp.broadcast_to(records[None], (half, REC_ROWS, 128)), axes, 0, 0, axis_index_groups=members
    ).reshape(half * REC_ROWS, 128)
    other = lax.ppermute(mine, axes, [(d, d ^ bit) for d in range(devices)])

    tiles_total = tiles_here * devices
    win_y = tiles_total // WIN_X
    off_x = (SCREEN_W - WIN_X * TILE_SIDE) // 2
    off_y = (SCREEN_H - win_y * TILE_SIDE) // 2
    sig_rows = devices * gauss_params.shape[1] // 128
    vmem = pl.BlockSpec(memory_space=pltpu.VMEM)
    smem = pl.BlockSpec(memory_space=pltpu.SMEM)
    pixel_colors, transmittance, partial_sig = pl.pallas_call(
        functools.partial(render_kernel, pair_bit, off_x, off_y),
        out_shape=(
            jax.ShapeDtypeStruct((tiles_here, 3, PIXELS), jnp.float32),
            jax.ShapeDtypeStruct((tiles_here, PIXELS), jnp.float32),
            jax.ShapeDtypeStruct((sig_rows, 128), jnp.float32),
        ),
        in_specs=[smem, smem, vmem, vmem, vmem],
        out_specs=(vmem, vmem, vmem),
        scratch_shapes=[
            pltpu.VMEM((PIECE_AT[-1] * 2 * devices, 256), jnp.bfloat16),
            pltpu.VMEM((32, PIXELS), jnp.bfloat16),
            pltpu.VMEM(((tiles_here + 1) * STRIDE, 128), jnp.float32),
            pltpu.VMEM(((tiles_here + 1) * STRIDE, 128), jnp.float32),
            pltpu.VMEM(((tiles_here + 1) * STRIDE, 128), jnp.float32),
            pltpu.VMEM(((tiles_here + 1) * STRIDE, 128), jnp.float32),
            pltpu.VMEM(((tiles_here + 1) * 16, CHUNK), jnp.bfloat16),
            pltpu.VMEM(((tiles_here + 1) * 16, PIXELS), jnp.float32),
            pltpu.VMEM((tiles_here * 2, 128), jnp.float32),
            pltpu.VMEM((tiles_here + 8, list_len), jnp.int32),
            pltpu.VMEM(((tiles_here + 1) * 32, CHUNK), jnp.bfloat16),
            pltpu.SMEM((tiles_here + UNROLL,), jnp.int32),
        ],
        compiler_params=pltpu.CompilerParams(vmem_limit_bytes=48 * 2**20),
    )(tile_ids, counts, mine, other, tile_lists)
    swapped = lax.all_to_all(partial_sig.reshape(devices, -1, 128), axes, 0, 0)
    significance = jnp.sum(swapped, axis=0).reshape(-1)
    return (pixel_colors, transmittance, significance)


def pair_bit_of(mesh):
    flat = list(mesh.devices.flat)
    bit = 0
    while (2 << bit) <= len(flat):
        if getattr(flat[0], "coords", 0) == getattr(flat[1 << bit], "coords", 1):
            return bit
        bit += 1
    return 0


def solution(mesh):
    return jax.shard_map(
        functools.partial(local, pair_bit_of(mesh)),
        mesh=mesh,
        in_specs=(P(None, ("blk", "row")), P(("blk", "row")), P(("blk", "row"), None)),
        out_specs=(P(("blk", "row"), None, None), P(("blk", "row"), None), P(("blk", "row"))),
        check_vma=False,
    )
```

```python
import functools

import jax
import jax.numpy as jnp
from jax import lax
from jax.experimental import pallas as pl
from jax.experimental.pallas import tpu as pltpu
from jax.sharding import PartitionSpec as P

TILE_SIDE = 16
SCREEN_W = 3840
SCREEN_H = 2160
WIN_X = 64
PIXELS = TILE_SIDE * TILE_SIDE
BLOCK = 128
UNROLL = 8
FIELDS = 9
REC_ROWS = 40
LOOKED = 2
PIECES = ((0, 0) + (2,) * 7)
PIECE_AT = tuple(sum(PIECES[:f]) for f in range(FIELDS + 1))
AXES = ("blk", "row")

FOCAL = 3200.0
DILATION = 0.3
SH_ZERO = 0.28209479177387814
ALPHA_CAP = 0.99
LOG2E = 1.4426950408889634
DARK = -200.0


def project_kernel(params_ref, lists_ref, rec_ref, count_ref):
    def row(index):
        return params_ref[index : index + 1, :]

    mean_x, mean_y, mean_z = row(0), row(1), row(2)
    scales = [jnp.exp(row(3 + k)) for k in range(3)]
    quat = [row(6 + k) for k in range(4)]
    norm = jnp.sqrt(quat[0] * quat[0] + quat[1] * quat[1] + quat[2] * quat[2] + quat[3] * quat[3])
    qw, qx, qy, qz = [q / norm for q in quat]
    rotation = [
        [1.0 - 2.0 * (qy * qy + qz * qz), 2.0 * (qx * qy - qw * qz), 2.0 * (qx * qz + qw * qy)],
        [2.0 * (qx * qy + qw * qz), 1.0 - 2.0 * (qx * qx + qz * qz), 2.0 * (qy * qz - qw * qx)],
        [2.0 * (qx * qz - qw * qy), 2.0 * (qy * qz + qw * qx), 1.0 - 2.0 * (qx * qx + qy * qy)],
    ]
    inv_z = 1.0 / mean_z
    jac_a = FOCAL * inv_z
    jac_x = -FOCAL * mean_x * inv_z * inv_z
    jac_y = -FOCAL * mean_y * inv_z * inv_z
    first = [(jac_a * rotation[0][k] + jac_x * rotation[2][k]) * scales[k] for k in range(3)]
    second = [(jac_a * rotation[1][k] + jac_y * rotation[2][k]) * scales[k] for k in range(3)]
    cov_a = first[0] * first[0] + first[1] * first[1] + first[2] * first[2] + DILATION
    cov_b = first[0] * second[0] + first[1] * second[1] + first[2] * second[2]
    cov_c = second[0] * second[0] + second[1] * second[1] + second[2] * second[2] + DILATION
    determinant = cov_a * cov_c - cov_b * cov_b
    logit = row(10)
    log_opacity = -LOG2E * (jnp.maximum(-logit, 0.0) + jnp.log1p(jnp.exp(-jnp.abs(logit))))
    fields = [
        FOCAL * mean_x * inv_z + SCREEN_W / 2,
        FOCAL * mean_y * inv_z + SCREEN_H / 2,
        (-0.5 * LOG2E) * (cov_c / determinant),
        LOG2E * (cov_b / determinant),
        (-0.5 * LOG2E) * (cov_a / determinant),
        jnp.maximum(log_opacity, DARK),
    ] + [jnp.maximum(SH_ZERO * row(11 + k) + 0.5, 0.0) for k in range(3)]
    rec_ref[...] = jnp.zeros_like(rec_ref)
    for f, value in enumerate(fields):
        for q in range(4):
            rec_ref[4 * f + q : 4 * f + q + 1, :] = value[:, 128 * q : 128 * (q + 1)]
    live = (lists_ref[...] >= 0).astype(jnp.int32)
    count_ref[...] = jnp.broadcast_to(jnp.sum(live, axis=1, keepdims=True), count_ref.shape)


def pieces_of(value, count):
    found = []
    for _ in range(count):
        piece = value.astype(jnp.bfloat16)
        found.append(piece)
        value = value - piece.astype(jnp.float32)
    return found


def bit_of(value, bit):
    return jnp.bitwise_and(jnp.right_shift(value, bit), 1)


def render_kernel(
    off_x, off_y, bits, tids_ref, count_ref, mine_ref, other_ref, lists_ref,
    color_ref, trans_ref, sig_ref,
    table_ref, feat_ref, a0_ref, a1_ref, w0_ref, w1_ref, coef_ref, rgb_ref, acc_ref,
    place_ref, ids_ref, block_ref,
):
    f32, bf16 = jnp.float32, jnp.bfloat16
    tiles, list_len = lists_ref.shape
    most = list_len // BLOCK
    half = mine_ref.shape[0] // REC_ROWS
    devices = 2 * half
    groups = tiles // 8
    stride = list_len + 8

    found = jnp.int32(0)
    longest = jnp.int32(0)
    for t in range(tiles):
        blocks = (count_ref[t, 0] + BLOCK - 1) // BLOCK
        longest = jnp.maximum(longest, blocks)
        for c in range(most):
            block_ref[found] = t * most + c
            found += (c < blocks).astype(jnp.int32)
    for i in range(UNROLL):
        block_ref[found + i] = tiles * most
    rounds = (found + UNROLL - 1) // UNROLL

    def tile_of(b):
        return lax.div(block_ref[b], most)

    def rows_of(b):
        return pl.ds(pl.multiple_of(block_ref[b] * BLOCK + tile_of(b) * 8, 8), BLOCK)

    def part_of(ref, b):
        return ref[pl.ds(block_ref[b], 1), :]

    me = lax.axis_index(AXES)
    core, far = bits
    ids = lists_ref[...]
    owner = jnp.right_shift(ids, 9)
    place = jnp.zeros_like(ids)
    at = 1
    for bit in range(devices.bit_length() - 1):
        value = bit_of(owner, bit)
        if bit == core:
            where = devices.bit_length() - 2
        elif bit == far:
            where = 0
        else:
            where, at = at, at + 1
        if bit in bits:
            value = jnp.bitwise_xor(value, bit_of(me, bit))
        place += jnp.left_shift(value, where)
    place = jnp.where(ids >= 0, place, -1)
    for value, ref in ((place, place_ref), (ids, ids_ref)):
        for c in range(most):
            ref[pl.ds(c, tiles, stride=most), :] = value[:, c * BLOCK : (c + 1) * BLOCK]
        ref[pl.ds(tiles * most, 8), :] = jnp.full((8, BLOCK), -1, jnp.int32)

    for f in range(FIELDS):
        for q in range(4 if PIECES[f] else 0):
            for part, ref in enumerate((mine_ref, other_ref)):
                rows = ref[pl.ds(4 * f + q, half, stride=REC_ROWS), :]
                for p, piece in enumerate(pieces_of(rows, PIECES[f])):
                    at = (PIECE_AT[f] + p) * 2 * devices + (q // 2) * devices + part * half
                    table_ref[pl.ds(at, half), pl.ds(128 * (q % 2), 128)] = piece

    pixel = lax.broadcasted_iota(jnp.int32, (8, PIXELS), 1)
    which = lax.broadcasted_iota(jnp.int32, (8, PIXELS), 0)
    px = jnp.bitwise_and(pixel, TILE_SIDE - 1).astype(f32) - 7.5
    py = jnp.right_shift(pixel, 4).astype(f32) - 7.5
    feats = jnp.zeros((8, PIXELS), f32)
    for j, value in enumerate((px * px, px * py, py * py, px, py, jnp.ones_like(px))):
        feats = jnp.where(which == j, value, feats)
    feat_ref[...] = jnp.concatenate([feats, feats, feats, jnp.zeros_like(feats)], axis=0).astype(bf16)

    acc_ref[...] = jnp.zeros_like(acc_ref)
    sig_ref[...] = jnp.zeros_like(sig_ref)
    for ref in (w0_ref, w1_ref):
        ref[pl.ds(tiles * stride, BLOCK), :] = jnp.zeros((BLOCK, 128), f32)

    def dark_body(t, _):
        def fill(c, _):
            at = pl.ds(pl.multiple_of(t * stride + c * BLOCK, 8), BLOCK)
            a0_ref[at, :] = jnp.zeros((BLOCK, 128), f32)
            a1_ref[at, :] = jnp.zeros((BLOCK, 128), f32)
            return 0

        return lax.fori_loop((count_ref[t, 0] + BLOCK - 1) // BLOCK, longest, fill, 0)

    lax.fori_loop(0, tiles, dark_body, 0)

    def one_hot(rows, index):
        iota = lax.broadcasted_iota(jnp.int32, (rows, index.shape[1]), 0)
        return (iota == index).astype(f32).astype(bf16)

    wide = 2 * BLOCK
    row8 = lax.broadcasted_iota(jnp.int32, (8, wide), 0)
    second = lax.broadcasted_iota(jnp.int32, (1, wide), 1) >= BLOCK

    def gather(pair):
        ids = jnp.concatenate([part_of(ids_ref, b) for b in pair], axis=1)
        place = jnp.concatenate([part_of(place_ref, b) for b in pair], axis=1)
        row = jnp.where(ids >= 0, bit_of(ids, 8) * devices + place, -1)
        chosen = lax.broadcasted_iota(jnp.int32, (2 * devices, wide), 0) == row
        looked = jnp.dot(table_ref[...], one_hot(256, jnp.bitwise_and(ids, 255)), preferred_element_type=f32)

        def fetch(f):
            total = None
            for p in range(PIECE_AT[f], PIECE_AT[f + 1]):
                piece = looked[p * 2 * devices : (p + 1) * 2 * devices]
                total = piece if total is None else total + piece
            best = jnp.zeros((8, wide), f32)
            for r in range(0, 2 * devices, 8):
                best = jnp.where(chosen[r : r + 8], total[r : r + 8], best)
            return jnp.sum(best, axis=0, keepdims=True)

        fields = []
        sub = lax.broadcasted_iota(jnp.int32, (8, BLOCK), 0)
        for f in range(0, LOOKED, 2):
            halves = []
            for j in range(2):
                here = jnp.broadcast_to(ids[:, BLOCK * j : BLOCK * (j + 1)], (8, BLOCK))
                owner = jnp.broadcast_to(place[:, BLOCK * j : BLOCK * (j + 1)], (8, BLOCK))
                lane = jnp.bitwise_and(here, 127)
                found = jnp.zeros((8, BLOCK), f32)
                for d in range(devices):
                    ref = mine_ref if d < half else other_ref
                    at = (d % half) * REC_ROWS + 4 * f
                    got = jnp.take_along_axis(ref[at : at + 8, :], lane, axis=1, mode="promise_in_bounds")
                    found = jnp.where(owner == d, got, found)
                quarter = jnp.bitwise_and(jnp.right_shift(here, 7), 3)
                halves.append(jnp.where(jnp.bitwise_and(sub, 3) == quarter, found, 0.0))
            both = jnp.concatenate(halves, axis=1)
            fields.append(jnp.sum(both[:4], axis=0, keepdims=True))
            fields.append(jnp.sum(both[4:], axis=0, keepdims=True))
        u, v, ca, cb, cc, log_op, red, green, blue = (fields + [fetch(f) for f in range(LOOKED, FIELDS)])[:FIELDS]
        tids = [tids_ref[jnp.minimum(tile_of(b), tiles - 1)] for b in pair]
        columns = [(off_x + TILE_SIDE // 2 + TILE_SIDE * jnp.bitwise_and(t, WIN_X - 1)).astype(f32) for t in tids]
        lines = [(off_y + TILE_SIDE // 2 + TILE_SIDE * jnp.right_shift(t, 6)).astype(f32) for t in tids]
        du = u - jnp.where(second, columns[1], columns[0])
        dv = v - jnp.where(second, lines[1], lines[0])
        log_op = jnp.where(ids >= 0, log_op, DARK)
        terms = (
            ca,
            cb,
            cc,
            -2.0 * ca * du - cb * dv,
            -2.0 * cc * dv - cb * du,
            ca * du * du + cc * dv * dv + cb * du * dv + log_op,
        )
        coef = jnp.zeros((8, wide), f32)
        for j, value in enumerate(terms):
            coef = jnp.where(row8 == j, value, coef)
        p0, p1, p2 = [p.astype(f32) for p in pieces_of(coef, 3)]
        coefs = jnp.concatenate([p0, p1, p2, jnp.zeros_like(p0)], axis=0).astype(bf16)
        rgb = jnp.zeros((8, wide), f32)
        for j, value in enumerate((red, green, blue)):
            rgb = jnp.where(row8 == j, value, rgb)
        colors = jnp.concatenate([p.astype(f32) for p in pieces_of(rgb, 2)], axis=0).astype(bf16)
        for j, b in enumerate(pair):
            lanes = slice(BLOCK * j, BLOCK * (j + 1))
            coef_ref[pl.ds(pl.multiple_of(b * 32, 32), 32), :] = coefs[:, lanes]
            rgb_ref[pl.ds(pl.multiple_of(b * 16, 16), 16), :] = colors[:, lanes]

    def gather_body(i, _):
        for j in range(0, UNROLL, 2):
            gather((i * UNROLL + j, i * UNROLL + j + 1))
        return 0

    lax.fori_loop(0, rounds, gather_body, 0)

    def alpha_body(i, _):
        for j in range(UNROLL):
            b = i * UNROLL + j
            exponent = lax.dot_general(
                coef_ref[pl.ds(pl.multiple_of(b * 32, 32), 32), :], feat_ref[...],
                (((0,), (0,)), ((), ())), preferred_element_type=f32,
            )
            alpha = jnp.minimum(jnp.exp2(exponent), ALPHA_CAP)
            a0_ref[rows_of(b), :] = alpha[:, :128]
            a1_ref[rows_of(b), :] = alpha[:, 128:]
        return 0

    lax.fori_loop(0, rounds, alpha_body, 0)

    def blend(step, through):
        for j in range(8):
            after = []
            for g in range(groups):
                for h, (a_ref, w_ref) in enumerate(((a0_ref, w0_ref), (a1_ref, w1_ref))):
                    at = pl.ds(g * 8 * stride + step * 8 + j, 8, stride=stride)
                    alpha = a_ref[at, :]
                    before = through[2 * g + h]
                    w_ref[at, :] = before * alpha
                    after.append(before * (1.0 - alpha))
            through = tuple(after)
        return through

    through = (jnp.ones((8, 128), f32),) * (2 * groups)
    through = lax.fori_loop(0, longest * (BLOCK // 8), blend, through)
    for g in range(groups):
        for h in range(2):
            trans_ref[8 * g : 8 * g + 8, 128 * h : 128 * (h + 1)] = through[2 * g + h]

    sig_rows = sig_ref.shape[0]

    def collect_body(i, _):
        left, right = [], []
        for j in range(UNROLL):
            b = i * UNROLL + j
            ids = part_of(ids_ref, b)
            w0, w1 = w0_ref[rows_of(b), :], w1_ref[rows_of(b), :]
            weights = jnp.concatenate(pieces_of(jnp.concatenate([w0, w1], axis=1), 2), axis=0)
            rgb = rgb_ref[pl.ds(pl.multiple_of(b * 16, 16), 16), :]
            at16 = pl.ds(pl.multiple_of(tile_of(b) * 16, 16), 16)
            acc_ref[at16, :] += jnp.dot(
                jnp.concatenate([rgb, rgb], axis=1), weights, preferred_element_type=f32
            )
            sums = jnp.sum((w0 + w1).T, axis=0, keepdims=True)
            hit = lax.broadcasted_iota(jnp.int32, (sig_rows, BLOCK), 0) == jnp.right_shift(ids, 7)
            left.append(
                jnp.concatenate(
                    [jnp.where(hit, p.astype(f32), 0.0).astype(bf16) for p in pieces_of(sums, 2)], axis=0
                )
            )
            right.append(one_hot(128, jnp.bitwise_and(ids, 127)))
        both = lax.dot_general(
            jnp.concatenate(left, axis=1), jnp.concatenate(right, axis=1), (((1,), (1,)), ((), ())),
            preferred_element_type=f32,
        )
        sig_ref[...] += both[:sig_rows] + both[sig_rows:]
        return 0

    lax.fori_loop(0, rounds, collect_body, 0)

    for t in range(tiles):
        color_ref[t] = acc_ref[16 * t : 16 * t + 3, :] + acc_ref[16 * t + 8 : 16 * t + 11, :]
    sig_ref[...] = sig_ref[...] * (1.0 / PIXELS)


def local(bits, gauss_params, tile_ids, tile_lists):
    devices = lax.axis_size(AXES)
    tiles_here, list_len = tile_lists.shape
    core, far = bits
    records, counts = pl.pallas_call(
        project_kernel,
        out_shape=(
            jax.ShapeDtypeStruct((REC_ROWS, 128), jnp.float32),
            jax.ShapeDtypeStruct((tiles_here, 128), jnp.int32),
        ),
    )(gauss_params, tile_lists)
    distant = lax.ppermute(records, AXES, [(d, d ^ (1 << far)) for d in range(devices)])
    room = tiles_here * list_len // BLOCK + max(UNROLL, 8)
    vmem = pl.BlockSpec(memory_space=pltpu.VMEM)
    smem = pl.BlockSpec(memory_space=pltpu.SMEM)
    fixed = (1 << core) | (1 << far)
    members = [
        [d for d in range(devices) if (d & fixed) == kind] for kind in (0, 1 << core, 1 << far, fixed)
    ]
    pair = jnp.stack([records, distant])
    ring = devices // 4
    mine = lax.all_to_all(
        jnp.broadcast_to(pair[None], (ring, 2, REC_ROWS, 128)), AXES, 0, 0, axis_index_groups=members
    ).reshape(2 * ring * REC_ROWS, 128)
    other = lax.ppermute(mine, AXES, [(d, d ^ (1 << core)) for d in range(devices)])

    tiles_total = tiles_here * devices
    win_y = tiles_total // WIN_X
    off_x = (SCREEN_W - WIN_X * TILE_SIDE) // 2
    off_y = (SCREEN_H - win_y * TILE_SIDE) // 2
    sig_rows = devices * gauss_params.shape[1] // 128
    entries = (tiles_here + 1) * (list_len + 8)
    pixel_colors, transmittance, partial_sig = pl.pallas_call(
        functools.partial(render_kernel, off_x, off_y, bits),
        out_shape=(
            jax.ShapeDtypeStruct((tiles_here, 3, PIXELS), jnp.float32),
            jax.ShapeDtypeStruct((tiles_here, PIXELS), jnp.float32),
            jax.ShapeDtypeStruct((sig_rows, 128), jnp.float32),
        ),
        in_specs=[smem, smem, vmem, vmem, vmem],
        out_specs=(vmem, vmem, vmem),
        scratch_shapes=[
            pltpu.VMEM((PIECE_AT[-1] * 2 * devices, 256), jnp.bfloat16),
            pltpu.VMEM((32, PIXELS), jnp.bfloat16),
            pltpu.VMEM((entries, 128), jnp.float32),
            pltpu.VMEM((entries, 128), jnp.float32),
            pltpu.VMEM((entries, 128), jnp.float32),
            pltpu.VMEM((entries, 128), jnp.float32),
            pltpu.VMEM((room * 32, BLOCK), jnp.bfloat16),
            pltpu.VMEM((room * 16, BLOCK), jnp.bfloat16),
            pltpu.VMEM(((tiles_here + 1) * 16, PIXELS), jnp.float32),
            pltpu.VMEM((room, BLOCK), jnp.int32),
            pltpu.VMEM((room, BLOCK), jnp.int32),
            pltpu.SMEM((room,), jnp.int32),
        ],
        compiler_params=pltpu.CompilerParams(vmem_limit_bytes=52 * 2**20),
    )(tile_ids, counts, mine, other, tile_lists)
    swapped = lax.all_to_all(partial_sig.reshape(devices, -1, 128), AXES, 0, 0)
    significance = jnp.sum(swapped, axis=0).reshape(-1)
    return (pixel_colors, transmittance, significance)


def bits_of(mesh):
    flat = list(mesh.devices.flat)
    places = [tuple(getattr(d, "coords", (0,))) for d in flat]

    def reach(bit):
        return sum(abs(p - q) for p, q in zip(places[0], places[1 << bit]))

    bits = range(len(flat).bit_length() - 1)
    core = min(bits, key=reach)
    far = max((b for b in bits if b != core), key=reach)
    return core, far


def solution(mesh):
    return jax.shard_map(
        functools.partial(local, bits_of(mesh)),
        mesh=mesh,
        in_specs=(P(None, AXES), P(AXES), P(AXES, None)),
        out_specs=(P(AXES, None, None), P(AXES, None), P(AXES)),
        check_vma=False,
    )
```

```python
import functools

import jax
import jax.numpy as jnp
from jax import lax
from jax.experimental import pallas as pl
from jax.experimental.pallas import tpu as pltpu
from jax.sharding import PartitionSpec as P

TILE_SIDE = 16
SCREEN_W = 3840
SCREEN_H = 2160
WIN_X = 64
PIXELS = TILE_SIDE * TILE_SIDE
BLOCK = 128
UNROLL = 8
GATHER_STEP = 32
ALPHA_STEP = 32
COLLECT_STEP = 32
FIELDS = 9
REC_ROWS = 40
LOOKED = 2
PIECES = ((0, 0) + (2,) * 7)
PIECE_AT = tuple(sum(PIECES[:f]) for f in range(FIELDS + 1))
AXES = ("blk", "row")

FOCAL = 3200.0
DILATION = 0.3
SH_ZERO = 0.28209479177387814
ALPHA_CAP = 0.99
LOG2E = 1.4426950408889634
DARK = -200.0


def project_kernel(params_ref, lists_ref, rec_ref, count_ref):
    def row(index):
        return params_ref[index : index + 1, :]

    mean_x, mean_y, mean_z = row(0), row(1), row(2)
    scales = [jnp.exp(row(3 + k)) for k in range(3)]
    quat = [row(6 + k) for k in range(4)]
    norm = jnp.sqrt(quat[0] * quat[0] + quat[1] * quat[1] + quat[2] * quat[2] + quat[3] * quat[3])
    qw, qx, qy, qz = [q / norm for q in quat]
    rotation = [
        [1.0 - 2.0 * (qy * qy + qz * qz), 2.0 * (qx * qy - qw * qz), 2.0 * (qx * qz + qw * qy)],
        [2.0 * (qx * qy + qw * qz), 1.0 - 2.0 * (qx * qx + qz * qz), 2.0 * (qy * qz - qw * qx)],
        [2.0 * (qx * qz - qw * qy), 2.0 * (qy * qz + qw * qx), 1.0 - 2.0 * (qx * qx + qy * qy)],
    ]
    inv_z = 1.0 / mean_z
    jac_a = FOCAL * inv_z
    jac_x = -FOCAL * mean_x * inv_z * inv_z
    jac_y = -FOCAL * mean_y * inv_z * inv_z
    first = [(jac_a * rotation[0][k] + jac_x * rotation[2][k]) * scales[k] for k in range(3)]
    second = [(jac_a * rotation[1][k] + jac_y * rotation[2][k]) * scales[k] for k in range(3)]
    cov_a = first[0] * first[0] + first[1] * first[1] + first[2] * first[2] + DILATION
    cov_b = first[0] * second[0] + first[1] * second[1] + first[2] * second[2]
    cov_c = second[0] * second[0] + second[1] * second[1] + second[2] * second[2] + DILATION
    determinant = cov_a * cov_c - cov_b * cov_b
    logit = row(10)
    log_opacity = -LOG2E * (jnp.maximum(-logit, 0.0) + jnp.log1p(jnp.exp(-jnp.abs(logit))))
    fields = [
        FOCAL * mean_x * inv_z + SCREEN_W / 2,
        FOCAL * mean_y * inv_z + SCREEN_H / 2,
        (-0.5 * LOG2E) * (cov_c / determinant),
        LOG2E * (cov_b / determinant),
        (-0.5 * LOG2E) * (cov_a / determinant),
        jnp.maximum(log_opacity, DARK),
    ] + [jnp.maximum(SH_ZERO * row(11 + k) + 0.5, 0.0) for k in range(3)]
    rec_ref[...] = jnp.zeros_like(rec_ref)
    for f, value in enumerate(fields):
        for q in range(4):
            rec_ref[4 * f + q : 4 * f + q + 1, :] = value[:, 128 * q : 128 * (q + 1)]
    live = (lists_ref[...] >= 0).astype(jnp.int32)
    count_ref[...] = jnp.broadcast_to(jnp.sum(live, axis=1, keepdims=True), count_ref.shape)


def pieces_of(value, count):
    found = []
    for _ in range(count):
        piece = value.astype(jnp.bfloat16)
        found.append(piece)
        value = value - piece.astype(jnp.float32)
    return found


def bit_of(value, bit):
    return jnp.bitwise_and(jnp.right_shift(value, bit), 1)


def render_kernel(
    off_x, off_y, bits, tids_ref, count_ref, mine_ref, other_ref, lists_ref,
    color_ref, trans_ref, sig_ref,
    table_ref, feat_ref, a0_ref, a1_ref, w0_ref, w1_ref, coef_ref, rgb_ref, acc_ref,
    place_ref, ids_ref, block_ref,
):
    f32, bf16 = jnp.float32, jnp.bfloat16
    tiles, list_len = lists_ref.shape
    most = list_len // BLOCK
    half = mine_ref.shape[0] // REC_ROWS
    devices = 2 * half
    groups = tiles // 8
    stride = list_len + 8

    found = jnp.int32(0)
    longest = jnp.int32(0)
    for t in range(tiles):
        blocks = (count_ref[t, 0] + BLOCK - 1) // BLOCK
        longest = jnp.maximum(longest, blocks)
        for c in range(most):
            block_ref[found] = t * most + c
            found += (c < blocks).astype(jnp.int32)
    for i in range(UNROLL):
        block_ref[found + i] = tiles * most

    def in_steps(body, size):
        whole = lax.div(found, size)
        lax.fori_loop(0, whole, lambda i, _: body(i * size, size), 0)
        rest = lax.div(found + UNROLL - 1, UNROLL)
        lax.fori_loop(whole * (size // UNROLL), rest, lambda i, _: body(i * UNROLL, UNROLL), 0)

    def tile_of(b):
        return lax.div(block_ref[b], most)

    def rows_of(b):
        return pl.ds(pl.multiple_of(block_ref[b] * BLOCK + tile_of(b) * 8, 8), BLOCK)

    def part_of(ref, b):
        return ref[pl.ds(block_ref[b], 1), :]

    me = lax.axis_index(AXES)
    core, far = bits
    ids = lists_ref[...]
    owner = jnp.right_shift(ids, 9)
    place = jnp.zeros_like(ids)
    at = 1
    for bit in range(devices.bit_length() - 1):
        value = bit_of(owner, bit)
        if bit == core:
            where = devices.bit_length() - 2
        elif bit == far:
            where = 0
        else:
            where, at = at, at + 1
        if bit in bits:
            value = jnp.bitwise_xor(value, bit_of(me, bit))
        place += jnp.left_shift(value, where)
    place = jnp.where(ids >= 0, place, -1)
    for value, ref in ((place, place_ref), (ids, ids_ref)):
        for c in range(most):
            ref[pl.ds(c, tiles, stride=most), :] = value[:, c * BLOCK : (c + 1) * BLOCK]
        ref[pl.ds(tiles * most, 8), :] = jnp.full((8, BLOCK), -1, jnp.int32)

    for f in range(FIELDS):
        for q in range(4 if PIECES[f] else 0):
            for part, ref in enumerate((mine_ref, other_ref)):
                rows = ref[pl.ds(4 * f + q, half, stride=REC_ROWS), :]
                for p, piece in enumerate(pieces_of(rows, PIECES[f])):
                    at = (PIECE_AT[f] + p) * 2 * devices + (q // 2) * devices + part * half
                    table_ref[pl.ds(at, half), pl.ds(128 * (q % 2), 128)] = piece

    pixel = lax.broadcasted_iota(jnp.int32, (8, PIXELS), 1)
    which = lax.broadcasted_iota(jnp.int32, (8, PIXELS), 0)
    px = jnp.bitwise_and(pixel, TILE_SIDE - 1).astype(f32) - 7.5
    py = jnp.right_shift(pixel, 4).astype(f32) - 7.5
    feats = jnp.zeros((8, PIXELS), f32)
    for j, value in enumerate((px * px, px * py, py * py, px, py, jnp.ones_like(px))):
        feats = jnp.where(which == j, value, feats)
    feat_ref[...] = jnp.concatenate([feats, feats, feats, jnp.zeros_like(feats)], axis=0).astype(bf16)

    acc_ref[...] = jnp.zeros_like(acc_ref)
    sig_ref[...] = jnp.zeros_like(sig_ref)
    for ref in (w0_ref, w1_ref):
        ref[pl.ds(tiles * stride, BLOCK), :] = jnp.zeros((BLOCK, 128), f32)

    def dark_body(t, _):
        def fill(c, _):
            at = pl.ds(pl.multiple_of(t * stride + c * BLOCK, 8), BLOCK)
            a0_ref[at, :] = jnp.zeros((BLOCK, 128), f32)
            a1_ref[at, :] = jnp.zeros((BLOCK, 128), f32)
            return 0

        return lax.fori_loop((count_ref[t, 0] + BLOCK - 1) // BLOCK, longest, fill, 0)

    lax.fori_loop(0, tiles, dark_body, 0)

    def one_hot(rows, index):
        iota = lax.broadcasted_iota(jnp.int32, (rows, index.shape[1]), 0)
        return (iota == index).astype(f32).astype(bf16)

    wide = 2 * BLOCK
    row8 = lax.broadcasted_iota(jnp.int32, (8, wide), 0)
    second = lax.broadcasted_iota(jnp.int32, (1, wide), 1) >= BLOCK

    def gather(pair):
        ids = jnp.concatenate([part_of(ids_ref, b) for b in pair], axis=1)
        place = jnp.concatenate([part_of(place_ref, b) for b in pair], axis=1)
        row = jnp.where(ids >= 0, bit_of(ids, 8) * devices + place, -1)
        chosen = lax.broadcasted_iota(jnp.int32, (2 * devices, wide), 0) == row
        looked = jnp.dot(table_ref[...], one_hot(256, jnp.bitwise_and(ids, 255)), preferred_element_type=f32)

        def fetch(f):
            total = None
            for p in range(PIECE_AT[f], PIECE_AT[f + 1]):
                piece = looked[p * 2 * devices : (p + 1) * 2 * devices]
                total = piece if total is None else total + piece
            best = jnp.zeros((8, wide), f32)
            for r in range(0, 2 * devices, 8):
                best = jnp.where(chosen[r : r + 8], total[r : r + 8], best)
            return jnp.sum(best, axis=0, keepdims=True)

        fields = []
        sub = lax.broadcasted_iota(jnp.int32, (8, BLOCK), 0)
        for f in range(0, LOOKED, 2):
            halves = []
            for j in range(2):
                here = jnp.broadcast_to(ids[:, BLOCK * j : BLOCK * (j + 1)], (8, BLOCK))
                owner = jnp.broadcast_to(place[:, BLOCK * j : BLOCK * (j + 1)], (8, BLOCK))
                lane = jnp.bitwise_and(here, 127)
                found = jnp.zeros((8, BLOCK), f32)
                for d in range(devices):
                    ref = mine_ref if d < half else other_ref
                    at = (d % half) * REC_ROWS + 4 * f
                    got = jnp.take_along_axis(ref[at : at + 8, :], lane, axis=1, mode="promise_in_bounds")
                    found = jnp.where(owner == d, got, found)
                quarter = jnp.bitwise_and(jnp.right_shift(here, 7), 3)
                halves.append(jnp.where(jnp.bitwise_and(sub, 3) == quarter, found, 0.0))
            both = jnp.concatenate(halves, axis=1)
            fields.append(jnp.sum(both[:4], axis=0, keepdims=True))
            fields.append(jnp.sum(both[4:], axis=0, keepdims=True))
        u, v, ca, cb, cc, log_op, red, green, blue = (fields + [fetch(f) for f in range(LOOKED, FIELDS)])[:FIELDS]
        tids = [tids_ref[jnp.minimum(tile_of(b), tiles - 1)] for b in pair]
        columns = [(off_x + TILE_SIDE // 2 + TILE_SIDE * jnp.bitwise_and(t, WIN_X - 1)).astype(f32) for t in tids]
        lines = [(off_y + TILE_SIDE // 2 + TILE_SIDE * jnp.right_shift(t, 6)).astype(f32) for t in tids]
        du = u - jnp.where(second, columns[1], columns[0])
        dv = v - jnp.where(second, lines[1], lines[0])
        log_op = jnp.where(ids >= 0, log_op, DARK)
        terms = (
            ca,
            cb,
            cc,
            -2.0 * ca * du - cb * dv,
            -2.0 * cc * dv - cb * du,
            ca * du * du + cc * dv * dv + cb * du * dv + log_op,
        )
        coef = jnp.zeros((8, wide), f32)
        for j, value in enumerate(terms):
            coef = jnp.where(row8 == j, value, coef)
        p0, p1, p2 = [p.astype(f32) for p in pieces_of(coef, 3)]
        coefs = jnp.concatenate([p0, p1, p2, jnp.zeros_like(p0)], axis=0).astype(bf16)
        rgb = jnp.zeros((8, wide), f32)
        for j, value in enumerate((red, green, blue)):
            rgb = jnp.where(row8 == j, value, rgb)
        colors = jnp.concatenate([p.astype(f32) for p in pieces_of(rgb, 2)], axis=0).astype(bf16)
        for j, b in enumerate(pair):
            lanes = slice(BLOCK * j, BLOCK * (j + 1))
            coef_ref[pl.ds(pl.multiple_of(b * 32, 32), 32), :] = coefs[:, lanes]
            rgb_ref[pl.ds(pl.multiple_of(b * 16, 16), 16), :] = colors[:, lanes]

    def gather_body(first, size):
        for j in range(0, size, 2):
            gather((first + j, first + j + 1))
        return 0

    in_steps(gather_body, GATHER_STEP)

    def alpha_body(first, size):
        for j in range(size):
            b = first + j
            exponent = lax.dot_general(
                coef_ref[pl.ds(pl.multiple_of(b * 32, 32), 32), :], feat_ref[...],
                (((0,), (0,)), ((), ())), preferred_element_type=f32,
            )
            alpha = jnp.minimum(jnp.exp2(exponent), ALPHA_CAP)
            a0_ref[rows_of(b), :] = alpha[:, :128]
            a1_ref[rows_of(b), :] = alpha[:, 128:]
        return 0

    in_steps(alpha_body, ALPHA_STEP)

    def blend(step, through):
        for j in range(8):
            after = []
            for g in range(groups):
                for h, (a_ref, w_ref) in enumerate(((a0_ref, w0_ref), (a1_ref, w1_ref))):
                    at = pl.ds(g * 8 * stride + step * 8 + j, 8, stride=stride)
                    alpha = a_ref[at, :]
                    before = through[2 * g + h]
                    w_ref[at, :] = before * alpha
                    after.append(before * (1.0 - alpha))
            through = tuple(after)
        return through

    through = (jnp.ones((8, 128), f32),) * (2 * groups)
    through = lax.fori_loop(0, longest * (BLOCK // 8), blend, through)
    for g in range(groups):
        for h in range(2):
            trans_ref[8 * g : 8 * g + 8, 128 * h : 128 * (h + 1)] = through[2 * g + h]

    sig_rows = sig_ref.shape[0]

    def collect_body(first, size):
        left, right = [], []
        for j in range(size):
            b = first + j
            ids = part_of(ids_ref, b)
            w0, w1 = w0_ref[rows_of(b), :], w1_ref[rows_of(b), :]
            weights = jnp.concatenate(pieces_of(jnp.concatenate([w0, w1], axis=1), 2), axis=0)
            rgb = rgb_ref[pl.ds(pl.multiple_of(b * 16, 16), 16), :]
            at16 = pl.ds(pl.multiple_of(tile_of(b) * 16, 16), 16)
            acc_ref[at16, :] += jnp.dot(
                jnp.concatenate([rgb, rgb], axis=1), weights, preferred_element_type=f32
            )
            sums = jnp.sum((w0 + w1).T, axis=0, keepdims=True)
            hit = lax.broadcasted_iota(jnp.int32, (sig_rows, BLOCK), 0) == jnp.right_shift(ids, 7)
            left.append(
                jnp.concatenate(
                    [jnp.where(hit, p.astype(f32), 0.0).astype(bf16) for p in pieces_of(sums, 2)], axis=0
                )
            )
            right.append(one_hot(128, jnp.bitwise_and(ids, 127)))
        both = lax.dot_general(
            jnp.concatenate(left, axis=1), jnp.concatenate(right, axis=1), (((1,), (1,)), ((), ())),
            preferred_element_type=f32,
        )
        sig_ref[...] += both[:sig_rows] + both[sig_rows:]
        return 0

    in_steps(collect_body, COLLECT_STEP)

    for t in range(tiles):
        color_ref[t] = acc_ref[16 * t : 16 * t + 3, :] + acc_ref[16 * t + 8 : 16 * t + 11, :]
    sig_ref[...] = sig_ref[...] * (1.0 / PIXELS)


def local(bits, gauss_params, tile_ids, tile_lists):
    devices = lax.axis_size(AXES)
    tiles_here, list_len = tile_lists.shape
    core, far = bits
    records, counts = pl.pallas_call(
        project_kernel,
        out_shape=(
            pltpu.VMEM((REC_ROWS, 128), jnp.float32),
            jax.ShapeDtypeStruct((tiles_here, 128), jnp.int32),
        ),
        out_specs=(pl.BlockSpec(memory_space=pltpu.VMEM),) * 2,
    )(gauss_params, tile_lists)
    distant = lax.ppermute(records, AXES, [(d, d ^ (1 << far)) for d in range(devices)])
    room = tiles_here * list_len // BLOCK + max(UNROLL, 8)
    vmem = pl.BlockSpec(memory_space=pltpu.VMEM)
    smem = pl.BlockSpec(memory_space=pltpu.SMEM)
    fixed = (1 << core) | (1 << far)
    members = [
        [d for d in range(devices) if (d & fixed) == kind] for kind in (0, 1 << core, 1 << far, fixed)
    ]
    pair = jnp.stack([records, distant])
    ring = devices // 4
    mine = lax.all_to_all(
        jnp.broadcast_to(pair[None], (ring, 2, REC_ROWS, 128)), AXES, 0, 0, axis_index_groups=members
    ).reshape(2 * ring * REC_ROWS, 128)
    other = lax.ppermute(mine, AXES, [(d, d ^ (1 << core)) for d in range(devices)])

    tiles_total = tiles_here * devices
    win_y = tiles_total // WIN_X
    off_x = (SCREEN_W - WIN_X * TILE_SIDE) // 2
    off_y = (SCREEN_H - win_y * TILE_SIDE) // 2
    sig_rows = devices * gauss_params.shape[1] // 128
    entries = (tiles_here + 1) * (list_len + 8)
    pixel_colors, transmittance, partial_sig = pl.pallas_call(
        functools.partial(render_kernel, off_x, off_y, bits),
        out_shape=(
            jax.ShapeDtypeStruct((tiles_here, 3, PIXELS), jnp.float32),
            jax.ShapeDtypeStruct((tiles_here, PIXELS), jnp.float32),
            jax.ShapeDtypeStruct((sig_rows, 128), jnp.float32),
        ),
        in_specs=[smem, smem, vmem, vmem, vmem],
        out_specs=(vmem, vmem, vmem),
        scratch_shapes=[
            pltpu.VMEM((PIECE_AT[-1] * 2 * devices, 256), jnp.bfloat16),
            pltpu.VMEM((32, PIXELS), jnp.bfloat16),
            pltpu.VMEM((entries, 128), jnp.float32),
            pltpu.VMEM((entries, 128), jnp.float32),
            pltpu.VMEM((entries, 128), jnp.float32),
            pltpu.VMEM((entries, 128), jnp.float32),
            pltpu.VMEM((room * 32, BLOCK), jnp.bfloat16),
            pltpu.VMEM((room * 16, BLOCK), jnp.bfloat16),
            pltpu.VMEM(((tiles_here + 1) * 16, PIXELS), jnp.float32),
            pltpu.VMEM((room, BLOCK), jnp.int32),
            pltpu.VMEM((room, BLOCK), jnp.int32),
            pltpu.SMEM((room,), jnp.int32),
        ],
        compiler_params=pltpu.CompilerParams(vmem_limit_bytes=52 * 2**20),
    )(tile_ids, counts, mine, other, tile_lists)
    swapped = lax.all_to_all(partial_sig.reshape(devices, -1, 128), AXES, 0, 0)
    significance = jnp.sum(swapped, axis=0).reshape(-1)
    return (pixel_colors, transmittance, significance)


def bits_of(mesh):
    flat = list(mesh.devices.flat)
    places = [tuple(getattr(d, "coords", (0,))) for d in flat]

    def reach(bit):
        return sum(abs(p - q) for p, q in zip(places[0], places[1 << bit]))

    bits = range(len(flat).bit_length() - 1)
    core = min(bits, key=reach)
    far = max((b for b in bits if b != core), key=reach)
    return core, far


def solution(mesh):
    return jax.shard_map(
        functools.partial(local, bits_of(mesh)),
        mesh=mesh,
        in_specs=(P(None, AXES), P(AXES), P(AXES, None)),
        out_specs=(P(AXES, None, None), P(AXES, None), P(AXES)),
        check_vma=False,
    )
```

```python
import functools

import jax
import jax.numpy as jnp
from jax import lax
from jax.experimental import pallas as pl
from jax.experimental.pallas import tpu as pltpu
from jax.sharding import PartitionSpec as P

TILE_SIDE = 16
SCREEN_W = 3840
SCREEN_H = 2160
WIN_X = 64
PIXELS = TILE_SIDE * TILE_SIDE
BLOCK = 128
UNROLL = 8
GATHER_STEP = 64
ALPHA_STEP = 64
COLLECT_STEP = 64
FIELDS = 9
REC_ROWS = 40
LOOKED = 2
PIECES = ((0, 0) + (2,) * 7)
PIECE_AT = tuple(sum(PIECES[:f]) for f in range(FIELDS + 1))
AXES = ("blk", "row")

FOCAL = 3200.0
DILATION = 0.3
SH_ZERO = 0.28209479177387814
ALPHA_CAP = 0.99
LOG2E = 1.4426950408889634
DARK = -200.0


def project_kernel(params_ref, lists_ref, rec_ref, count_ref):
    def row(index):
        return params_ref[index : index + 1, :]

    mean_x, mean_y, mean_z = row(0), row(1), row(2)
    scales = [jnp.exp(row(3 + k)) for k in range(3)]
    quat = [row(6 + k) for k in range(4)]
    norm = jnp.sqrt(quat[0] * quat[0] + quat[1] * quat[1] + quat[2] * quat[2] + quat[3] * quat[3])
    qw, qx, qy, qz = [q / norm for q in quat]
    rotation = [
        [1.0 - 2.0 * (qy * qy + qz * qz), 2.0 * (qx * qy - qw * qz), 2.0 * (qx * qz + qw * qy)],
        [2.0 * (qx * qy + qw * qz), 1.0 - 2.0 * (qx * qx + qz * qz), 2.0 * (qy * qz - qw * qx)],
        [2.0 * (qx * qz - qw * qy), 2.0 * (qy * qz + qw * qx), 1.0 - 2.0 * (qx * qx + qy * qy)],
    ]
    inv_z = 1.0 / mean_z
    jac_a = FOCAL * inv_z
    jac_x = -FOCAL * mean_x * inv_z * inv_z
    jac_y = -FOCAL * mean_y * inv_z * inv_z
    first = [(jac_a * rotation[0][k] + jac_x * rotation[2][k]) * scales[k] for k in range(3)]
    second = [(jac_a * rotation[1][k] + jac_y * rotation[2][k]) * scales[k] for k in range(3)]
    cov_a = first[0] * first[0] + first[1] * first[1] + first[2] * first[2] + DILATION
    cov_b = first[0] * second[0] + first[1] * second[1] + first[2] * second[2]
    cov_c = second[0] * second[0] + second[1] * second[1] + second[2] * second[2] + DILATION
    determinant = cov_a * cov_c - cov_b * cov_b
    logit = row(10)
    log_opacity = -LOG2E * (jnp.maximum(-logit, 0.0) + jnp.log1p(jnp.exp(-jnp.abs(logit))))
    fields = [
        FOCAL * mean_x * inv_z + SCREEN_W / 2,
        FOCAL * mean_y * inv_z + SCREEN_H / 2,
        (-0.5 * LOG2E) * (cov_c / determinant),
        LOG2E * (cov_b / determinant),
        (-0.5 * LOG2E) * (cov_a / determinant),
        jnp.maximum(log_opacity, DARK),
    ] + [jnp.maximum(SH_ZERO * row(11 + k) + 0.5, 0.0) for k in range(3)]
    rec_ref[...] = jnp.zeros_like(rec_ref)
    for f, value in enumerate(fields):
        for q in range(4):
            rec_ref[4 * f + q : 4 * f + q + 1, :] = value[:, 128 * q : 128 * (q + 1)]
    live = (lists_ref[...] >= 0).astype(jnp.int32)
    count_ref[...] = jnp.broadcast_to(jnp.sum(live, axis=1, keepdims=True), count_ref.shape)


def pieces_of(value, count):
    found = []
    for _ in range(count):
        piece = value.astype(jnp.bfloat16)
        found.append(piece)
        value = value - piece.astype(jnp.float32)
    return found


def bit_of(value, bit):
    return jnp.bitwise_and(jnp.right_shift(value, bit), 1)


def render_kernel(
    off_x, off_y, bits, tids_ref, count_ref, mine_ref, other_ref, lists_ref,
    color_ref, trans_ref, sig_ref,
    table_ref, feat_ref, a0_ref, a1_ref, w0_ref, w1_ref, coef_ref, rgb_ref, acc_ref,
    place_ref, ids_ref, block_ref,
):
    f32, bf16 = jnp.float32, jnp.bfloat16
    tiles, list_len = lists_ref.shape
    most = list_len // BLOCK
    half = mine_ref.shape[0] // REC_ROWS
    devices = 2 * half
    groups = tiles // 8
    stride = list_len + 8

    found = jnp.int32(0)
    longest = jnp.int32(0)
    for t in range(tiles):
        blocks = (count_ref[t, 0] + BLOCK - 1) // BLOCK
        longest = jnp.maximum(longest, blocks)
        for c in range(most):
            block_ref[found] = t * most + c
            found += (c < blocks).astype(jnp.int32)
    for i in range(UNROLL):
        block_ref[found + i] = tiles * most

    def in_steps(body, size):
        units = lax.div(found + UNROLL - 1, UNROLL)
        done = 0
        while size >= UNROLL:
            share = size // UNROLL
            first = done // share if isinstance(done, int) else lax.div(done, share)
            last = lax.div(units, share)
            lax.fori_loop(first, last, lambda i, _, size=size: body(i * size, size), 0)
            done = last * share
            size //= 2

    def tile_of(b):
        return lax.div(block_ref[b], most)

    def rows_of(b):
        return pl.ds(pl.multiple_of(block_ref[b] * BLOCK + tile_of(b) * 8, 8), BLOCK)

    def part_of(ref, b):
        return ref[pl.ds(block_ref[b], 1), :]

    me = lax.axis_index(AXES)
    core, far = bits
    ids = lists_ref[...]
    owner = jnp.right_shift(ids, 9)
    place = jnp.zeros_like(ids)
    at = 1
    for bit in range(devices.bit_length() - 1):
        value = bit_of(owner, bit)
        if bit == core:
            where = devices.bit_length() - 2
        elif bit == far:
            where = 0
        else:
            where, at = at, at + 1
        if bit in bits:
            value = jnp.bitwise_xor(value, bit_of(me, bit))
        place += jnp.left_shift(value, where)
    place = jnp.where(ids >= 0, place, -1)
    for value, ref in ((place, place_ref), (ids, ids_ref)):
        for c in range(most):
            ref[pl.ds(c, tiles, stride=most), :] = value[:, c * BLOCK : (c + 1) * BLOCK]
        ref[pl.ds(tiles * most, 8), :] = jnp.full((8, BLOCK), -1, jnp.int32)

    for f in range(FIELDS):
        for q in range(4 if PIECES[f] else 0):
            for part, ref in enumerate((mine_ref, other_ref)):
                rows = ref[pl.ds(4 * f + q, half, stride=REC_ROWS), :]
                for p, piece in enumerate(pieces_of(rows, PIECES[f])):
                    at = (PIECE_AT[f] + p) * 2 * devices + (q // 2) * devices + part * half
                    table_ref[pl.ds(at, half), pl.ds(128 * (q % 2), 128)] = piece

    pixel = lax.broadcasted_iota(jnp.int32, (8, PIXELS), 1)
    which = lax.broadcasted_iota(jnp.int32, (8, PIXELS), 0)
    px = jnp.bitwise_and(pixel, TILE_SIDE - 1).astype(f32) - 7.5
    py = jnp.right_shift(pixel, 4).astype(f32) - 7.5
    feats = jnp.zeros((8, PIXELS), f32)
    for j, value in enumerate((px * px, px * py, py * py, px, py, jnp.ones_like(px))):
        feats = jnp.where(which == j, value, feats)
    feat_ref[...] = jnp.concatenate([feats, feats, feats, jnp.zeros_like(feats)], axis=0).astype(bf16)

    acc_ref[...] = jnp.zeros_like(acc_ref)
    sig_ref[...] = jnp.zeros_like(sig_ref)
    for ref in (w0_ref, w1_ref):
        ref[pl.ds(tiles * stride, BLOCK), :] = jnp.zeros((BLOCK, 128), f32)

    def dark_body(t, _):
        def fill(c, _):
            at = pl.ds(pl.multiple_of(t * stride + c * BLOCK, 8), BLOCK)
            a0_ref[at, :] = jnp.zeros((BLOCK, 128), f32)
            a1_ref[at, :] = jnp.zeros((BLOCK, 128), f32)
            return 0

        return lax.fori_loop((count_ref[t, 0] + BLOCK - 1) // BLOCK, longest, fill, 0)

    lax.fori_loop(0, tiles, dark_body, 0)

    def one_hot(rows, index):
        here = jnp.where((index >= 0) & (index < rows), index, -1).astype(f32).astype(bf16)
        iota = lax.broadcasted_iota(jnp.int32, (rows, index.shape[1]), 0).astype(f32).astype(bf16)
        return jnp.where(iota == here, jnp.array(1, bf16), jnp.array(0, bf16))

    wide = 2 * BLOCK
    row8 = lax.broadcasted_iota(jnp.int32, (8, wide), 0)
    second = lax.broadcasted_iota(jnp.int32, (1, wide), 1) >= BLOCK

    def gather(pair):
        ids = jnp.concatenate([part_of(ids_ref, b) for b in pair], axis=1)
        place = jnp.concatenate([part_of(place_ref, b) for b in pair], axis=1)
        row = jnp.where(ids >= 0, bit_of(ids, 8) * devices + place, -1)
        chosen = lax.broadcasted_iota(jnp.int32, (2 * devices, wide), 0) == row
        looked = jnp.dot(table_ref[...], one_hot(256, jnp.bitwise_and(ids, 255)), preferred_element_type=f32)

        def fetch(f):
            total = None
            for p in range(PIECE_AT[f], PIECE_AT[f + 1]):
                piece = looked[p * 2 * devices : (p + 1) * 2 * devices]
                total = piece if total is None else total + piece
            best = jnp.zeros((8, wide), f32)
            for r in range(0, 2 * devices, 8):
                best = jnp.where(chosen[r : r + 8], total[r : r + 8], best)
            return jnp.sum(best, axis=0, keepdims=True)

        fields = []
        sub = lax.broadcasted_iota(jnp.int32, (8, BLOCK), 0)
        for f in range(0, LOOKED, 2):
            halves = []
            for j in range(2):
                here = jnp.broadcast_to(ids[:, BLOCK * j : BLOCK * (j + 1)], (8, BLOCK))
                owner = jnp.broadcast_to(place[:, BLOCK * j : BLOCK * (j + 1)], (8, BLOCK))
                lane = jnp.bitwise_and(here, 127)
                found = jnp.zeros((8, BLOCK), f32)
                for d in range(devices):
                    ref = mine_ref if d < half else other_ref
                    at = (d % half) * REC_ROWS + 4 * f
                    got = jnp.take_along_axis(ref[at : at + 8, :], lane, axis=1, mode="promise_in_bounds")
                    found = jnp.where(owner == d, got, found)
                quarter = jnp.bitwise_and(jnp.right_shift(here, 7), 3)
                halves.append(jnp.where(jnp.bitwise_and(sub, 3) == quarter, found, 0.0))
            both = jnp.concatenate(halves, axis=1)
            fields.append(jnp.sum(both[:4], axis=0, keepdims=True))
            fields.append(jnp.sum(both[4:], axis=0, keepdims=True))
        u, v, ca, cb, cc, log_op, red, green, blue = (fields + [fetch(f) for f in range(LOOKED, FIELDS)])[:FIELDS]
        tids = [tids_ref[jnp.minimum(tile_of(b), tiles - 1)] for b in pair]
        columns = [(off_x + TILE_SIDE // 2 + TILE_SIDE * jnp.bitwise_and(t, WIN_X - 1)).astype(f32) for t in tids]
        lines = [(off_y + TILE_SIDE // 2 + TILE_SIDE * jnp.right_shift(t, 6)).astype(f32) for t in tids]
        du = u - jnp.where(second, columns[1], columns[0])
        dv = v - jnp.where(second, lines[1], lines[0])
        log_op = jnp.where(ids >= 0, log_op, DARK)
        terms = (
            ca,
            cb,
            cc,
            -2.0 * ca * du - cb * dv,
            -2.0 * cc * dv - cb * du,
            ca * du * du + cc * dv * dv + cb * du * dv + log_op,
        )
        coef = jnp.zeros((8, wide), f32)
        for j, value in enumerate(terms):
            coef = jnp.where(row8 == j, value, coef)
        p0, p1, p2 = [p.astype(f32) for p in pieces_of(coef, 3)]
        coefs = jnp.concatenate([p0, p1, p2, jnp.zeros_like(p0)], axis=0).astype(bf16)
        rgb = jnp.zeros((8, wide), f32)
        for j, value in enumerate((red, green, blue)):
            rgb = jnp.where(row8 == j, value, rgb)
        colors = jnp.concatenate([p.astype(f32) for p in pieces_of(rgb, 2)], axis=0).astype(bf16)
        for j, b in enumerate(pair):
            lanes = slice(BLOCK * j, BLOCK * (j + 1))
            coef_ref[pl.ds(pl.multiple_of(b * 32, 32), 32), :] = coefs[:, lanes]
            rgb_ref[pl.ds(pl.multiple_of(b * 16, 16), 16), :] = colors[:, lanes]

    def gather_body(first, size):
        for j in range(0, size, 2):
            gather((first + j, first + j + 1))
        return 0

    in_steps(gather_body, GATHER_STEP)

    def alpha_body(first, size):
        for j in range(size):
            b = first + j
            exponent = lax.dot_general(
                coef_ref[pl.ds(pl.multiple_of(b * 32, 32), 32), :], feat_ref[...],
                (((0,), (0,)), ((), ())), preferred_element_type=f32,
            )
            alpha = jnp.minimum(jnp.exp2(exponent), ALPHA_CAP)
            a0_ref[rows_of(b), :] = alpha[:, :128]
            a1_ref[rows_of(b), :] = alpha[:, 128:]
        return 0

    in_steps(alpha_body, ALPHA_STEP)

    def blend(step, through):
        for j in range(8):
            after = []
            for g in range(groups):
                for h, (a_ref, w_ref) in enumerate(((a0_ref, w0_ref), (a1_ref, w1_ref))):
                    at = pl.ds(g * 8 * stride + step * 8 + j, 8, stride=stride)
                    alpha = a_ref[at, :]
                    before = through[2 * g + h]
                    w_ref[at, :] = before * alpha
                    after.append(before * (1.0 - alpha))
            through = tuple(after)
        return through

    through = (jnp.ones((8, 128), f32),) * (2 * groups)
    through = lax.fori_loop(0, longest * (BLOCK // 8), blend, through)
    for g in range(groups):
        for h in range(2):
            trans_ref[8 * g : 8 * g + 8, 128 * h : 128 * (h + 1)] = through[2 * g + h]

    sig_rows = sig_ref.shape[0]

    def collect_body(first, size):
        left, right = [], []
        for j in range(size):
            b = first + j
            ids = part_of(ids_ref, b)
            w0, w1 = w0_ref[rows_of(b), :], w1_ref[rows_of(b), :]
            weights = jnp.concatenate(pieces_of(jnp.concatenate([w0, w1], axis=1), 2), axis=0)
            rgb = rgb_ref[pl.ds(pl.multiple_of(b * 16, 16), 16), :]
            at16 = pl.ds(pl.multiple_of(tile_of(b) * 16, 16), 16)
            acc_ref[at16, :] += jnp.dot(
                jnp.concatenate([rgb, rgb], axis=1), weights, preferred_element_type=f32
            )
            sums = jnp.sum((w0 + w1).T, axis=0, keepdims=True)
            hit = lax.broadcasted_iota(jnp.int32, (sig_rows, BLOCK), 0) == jnp.right_shift(ids, 7)
            left.append(
                jnp.concatenate(
                    [jnp.where(hit, p.astype(f32), 0.0).astype(bf16) for p in pieces_of(sums, 2)], axis=0
                )
            )
            right.append(one_hot(128, jnp.bitwise_and(ids, 127)))
        both = lax.dot_general(
            jnp.concatenate(left, axis=1), jnp.concatenate(right, axis=1), (((1,), (1,)), ((), ())),
            preferred_element_type=f32,
        )
        sig_ref[...] += both[:sig_rows] + both[sig_rows:]
        return 0

    in_steps(collect_body, COLLECT_STEP)

    for t in range(tiles):
        color_ref[t] = acc_ref[16 * t : 16 * t + 3, :] + acc_ref[16 * t + 8 : 16 * t + 11, :]
    sig_ref[...] = sig_ref[...] * (1.0 / PIXELS)


def local(bits, gauss_params, tile_ids, tile_lists):
    devices = lax.axis_size(AXES)
    tiles_here, list_len = tile_lists.shape
    core, far = bits
    records, counts = pl.pallas_call(
        project_kernel,
        out_shape=(
            pltpu.VMEM((REC_ROWS, 128), jnp.float32),
            jax.ShapeDtypeStruct((tiles_here, 128), jnp.int32),
        ),
        out_specs=(pl.BlockSpec(memory_space=pltpu.VMEM),) * 2,
    )(gauss_params, tile_lists)
    distant = lax.ppermute(records, AXES, [(d, d ^ (1 << far)) for d in range(devices)])
    room = tiles_here * list_len // BLOCK + max(UNROLL, 8)
    vmem = pl.BlockSpec(memory_space=pltpu.VMEM)
    smem = pl.BlockSpec(memory_space=pltpu.SMEM)
    fixed = (1 << core) | (1 << far)
    members = [
        [d for d in range(devices) if (d & fixed) == kind] for kind in (0, 1 << core, 1 << far, fixed)
    ]
    pair = jnp.stack([records, distant])
    ring = devices // 4
    mine = lax.all_to_all(
        jnp.broadcast_to(pair[None], (ring, 2, REC_ROWS, 128)), AXES, 0, 0, axis_index_groups=members
    ).reshape(2 * ring * REC_ROWS, 128)
    other = lax.ppermute(mine, AXES, [(d, d ^ (1 << core)) for d in range(devices)])

    tiles_total = tiles_here * devices
    win_y = tiles_total // WIN_X
    off_x = (SCREEN_W - WIN_X * TILE_SIDE) // 2
    off_y = (SCREEN_H - win_y * TILE_SIDE) // 2
    sig_rows = devices * gauss_params.shape[1] // 128
    entries = (tiles_here + 1) * (list_len + 8)
    pixel_colors, transmittance, partial_sig = pl.pallas_call(
        functools.partial(render_kernel, off_x, off_y, bits),
        out_shape=(
            jax.ShapeDtypeStruct((tiles_here, 3, PIXELS), jnp.float32),
            jax.ShapeDtypeStruct((tiles_here, PIXELS), jnp.float32),
            jax.ShapeDtypeStruct((sig_rows, 128), jnp.float32),
        ),
        in_specs=[smem, smem, vmem, vmem, vmem],
        out_specs=(vmem, vmem, vmem),
        scratch_shapes=[
            pltpu.VMEM((PIECE_AT[-1] * 2 * devices, 256), jnp.bfloat16),
            pltpu.VMEM((32, PIXELS), jnp.bfloat16),
            pltpu.VMEM((entries, 128), jnp.float32),
            pltpu.VMEM((entries, 128), jnp.float32),
            pltpu.VMEM((entries, 128), jnp.float32),
            pltpu.VMEM((entries, 128), jnp.float32),
            pltpu.VMEM((room * 32, BLOCK), jnp.bfloat16),
            pltpu.VMEM((room * 16, BLOCK), jnp.bfloat16),
            pltpu.VMEM(((tiles_here + 1) * 16, PIXELS), jnp.float32),
            pltpu.VMEM((room, BLOCK), jnp.int32),
            pltpu.VMEM((room, BLOCK), jnp.int32),
            pltpu.SMEM((room,), jnp.int32),
        ],
        compiler_params=pltpu.CompilerParams(vmem_limit_bytes=52 * 2**20),
    )(tile_ids, counts, mine, other, tile_lists)
    swapped = lax.all_to_all(partial_sig.reshape(devices, -1, 128), AXES, 0, 0)
    significance = jnp.sum(swapped, axis=0).reshape(-1)
    return (pixel_colors, transmittance, significance)


def bits_of(mesh):
    flat = list(mesh.devices.flat)
    places = [tuple(getattr(d, "coords", (0,))) for d in flat]

    def reach(bit):
        return sum(abs(p - q) for p, q in zip(places[0], places[1 << bit]))

    bits = range(len(flat).bit_length() - 1)
    core = min(bits, key=reach)
    far = max((b for b in bits if b != core), key=reach)
    return core, far


def solution(mesh):
    return jax.shard_map(
        functools.partial(local, bits_of(mesh)),
        mesh=mesh,
        in_specs=(P(None, AXES), P(AXES), P(AXES, None)),
        out_specs=(P(AXES, None, None), P(AXES, None), P(AXES)),
        check_vma=False,
    )
```
